32 devices in a mesh: dp: 8 (over z, y), tensor: 4 (over x, core).
Axes of the slice: x: 2, y: 2, z: 4, core: 2. Of those that a mesh axis runs over, the one named last changes fastest.
Arguments:
- tokens: bfloat16 [1024, 8192], P(('dp', 'tensor')), may hold values from -6 to 6
- base_weight: bfloat16 [8192, 4096], P(None, 'tensor'), may hold values from -0.0625 to 0.0625
- out_grad: bfloat16 [1024, 4096], P('dp', 'tensor'), may hold values from -6 to 6
- block_index: int32 [8, 2], replicated, may hold values from 0 to 63, as said below
- block_owner: int32 [8], replicated, may hold values from 0 to 7, as said below
- delta: bfloat16 [16, 16384], P('dp', 'tensor'), may hold values from -0.5 to 0.5
- moment1: float32 [16, 16384], P('dp', 'tensor'), may hold values from -4 to 4
- moment2: float32 [16, 16384], P('dp', 'tensor'), may hold values from 0.01 to 1
Outputs:
- projected: bfloat16 [1024, 4096], P('dp', 'tensor')
- input_grad: bfloat16 [1024, 8192], P(('dp', 'tensor'))
- new_delta: bfloat16 [16, 16384], P('dp', 'tensor')
- new_moment1: float32 [16, 16384], P('dp', 'tensor')
- new_moment2: float32 [16, 16384], P('dp', 'tensor')
The draws below stay inside these ranges and needn't reach their ends.
Inputs may be any that keep to these rules, and one draw needn't show every extreme that they name: `block_index`: the pairs (row block, head) are all different; row blocks are below D / 128 and heads below 32. `block_owner`: each owner holds at most 2 blocks and some owner exactly 2; some owners hold none.
All inputs are finite; a program needn't handle non-finite values.
Results may differ from the reference program's by a relative error of at most 0.013.
Values may be sent and summed in bfloat16 or wider, within the bound.
No kernel may reach another device: no remote copies, remote signals or barrier semaphores. Data moves between devices by JAX's collectives and lax.ppermute only.
A program may use at most 128 MiB of HBM per device.

```python
import math
import jax
import jax.numpy as jnp
from jax import lax

D = 8192
HEAD_DIM = 128
HEADS = 32
BPO = 1
CAP = 2
NB = 8
SLOTS = 16
TOKENS = 1024
N_DP = 8
N_TENSOR = 4


def move_front(order, target, place):
    cells = order.shape[0]
    where_now = jnp.sum(jnp.where(order == target, jnp.arange(cells, dtype=jnp.int32), 0)).astype(jnp.int32)
    held = order[place]
    order = order.at[where_now].set(held)
    return order.at[place].set(target)


def draw_block_index(key, part):
    cells = D // HEAD_DIM * HEADS
    order = jax.random.permutation(jax.random.fold_in(key, 11), cells).astype(jnp.int32)
    far_cell = jnp.int32(cells - 1)
    near_cell = jnp.int32(0)
    order = move_front(order, far_cell, 0)
    order = move_front(order, near_cell, 1)
    order = order[:NB]
    return jnp.stack([order // HEADS, order % HEADS], axis=1).astype(jnp.int32)


def draw_block_owner(key, part):
    owners = jnp.arange(N_DP, dtype=jnp.int32)
    phase = owners % 4
    counts = jnp.where(phase == 0, 2 * BPO, jnp.where(phase == 3, 0, BPO))
    sorted_owner = jnp.repeat(owners, counts, total_repeat_length=NB)
    relabel = jax.random.permutation(jax.random.fold_in(key, 21), N_DP)
    shuffle = jax.random.permutation(jax.random.fold_in(key, 22), NB)
    return relabel[sorted_owner][shuffle].astype(jnp.int32)


def levels(key, dims, cuts, smallest, top_value):
    def one(axis_at, shards_of):
        draws = jax.random.uniform(jax.random.fold_in(jax.random.fold_in(key, 6), axis_at), (shards_of,), jnp.float32, smallest / len(cuts), top_value / len(cuts))
        return jnp.repeat(jnp.exp(draws), dims[axis_at] // shards_of).reshape((-1,) + (1,) * (len(dims) - axis_at - 1))

    level = one(*cuts[0])
    for cut in cuts[1:]:
        level = level * one(*cut)
    return level


def centred(own_key, shape, width, reach, cuts=(), kind=jnp.bfloat16):
    factor_of = levels(own_key, shape, cuts, -0.22, 0.18) if cuts else 1.0
    entries = jax.random.normal(own_key, shape, jnp.float32) * width * factor_of
    return jnp.minimum(jnp.maximum(entries, -reach), reach).astype(kind)


def setup_inputs(seed: int = 0) -> dict:
    key_list = jax.random.split(jax.random.key(seed), 9)
    return {
        "tokens": centred(key_list[0], (TOKENS, D), 1.0, 6.0, ((0, 32),)),
        "base_weight": centred(key_list[1], (D, HEADS * HEAD_DIM), D ** -0.5, 0.0625, ((1, 4),)),
        "out_grad": centred(key_list[2], (TOKENS, HEADS * HEAD_DIM), 1.0, 6.0, ((0, 8), (1, 4))),
        "block_index": draw_block_index(jax.random.fold_in(key_list[8], 71), 0),
        "block_owner": draw_block_owner(jax.random.fold_in(key_list[8], 71), 0),
        "delta": centred(key_list[5], (SLOTS, HEAD_DIM * HEAD_DIM), HEAD_DIM ** -0.5, 0.5, ((0, 8), (1, 4))),
        "moment1": centred(key_list[6], (SLOTS, HEAD_DIM * HEAD_DIM), 0.5, 4.0, ((0, 8), (1, 4)), jnp.float32),
        "moment2": jnp.clip(jnp.exp(math.log(1.0) - 4.6051702 * jax.random.uniform(key_list[7], (SLOTS, HEAD_DIM * HEAD_DIM), jnp.float32) ** levels(key_list[7], (SLOTS, HEAD_DIM * HEAD_DIM), ((0, 8), (1, 4)), -0.2, 0.2)), 0.01, 1.0),
    }


CORRECT_ONE = 1.0 - 0.9 ** 10
CORRECT_TWO = 1.0 - 0.999 ** 10

def tables(block_index, block_owner):
    owners = jnp.arange(N_DP, dtype=jnp.int32)
    owner_hit = (block_owner[:, None] == owners[None, :]).astype(jnp.int32)
    before = jnp.cumsum(owner_hit, axis=0) - owner_hit
    slot_rank = lax.optimization_barrier(jnp.sum(before * owner_hit, axis=1))
    slot_of = block_owner * CAP + slot_rank
    slot_match = (slot_of[None, :] == jnp.arange(SLOTS, dtype=jnp.int32)[:, None]).astype(jnp.int32)
    slot_live = lax.optimization_barrier(jnp.sum(slot_match, axis=1))
    slot_row = lax.optimization_barrier(jnp.sum(slot_match * block_index[None, :, 0], axis=1))
    slot_head = lax.optimization_barrier(jnp.sum(slot_match * block_index[None, :, 1], axis=1))
    return (slot_live, slot_row, slot_head)

def reference(tokens, base_weight, out_grad, block_index, block_owner, delta, moment1, moment2):
    slot_live, slot_row, slot_head = tables(block_index, block_owner)
    blocks = delta.reshape(SLOTS, HEAD_DIM, HEAD_DIM)
    base_part = jnp.dot(tokens, base_weight, preferred_element_type=jnp.float32)

    def add_forward(slot_index, running):
        token_slab = lax.dynamic_slice_in_dim(tokens, slot_row[slot_index] * HEAD_DIM, HEAD_DIM, 1)
        delta_term = jnp.dot(token_slab, blocks[slot_index], preferred_element_type=jnp.float32)
        delta_term = delta_term * slot_live[slot_index].astype(jnp.float32)
        column = slot_head[slot_index] * HEAD_DIM
        current = lax.dynamic_slice_in_dim(running, column, HEAD_DIM, 1)
        return lax.dynamic_update_slice_in_dim(running, current + delta_term, column, 1)
    projected = lax.fori_loop(0, SLOTS, add_forward, base_part).astype(jnp.bfloat16)
    heads_dev = HEADS // N_TENSOR
    width_dev = heads_dev * HEAD_DIM
    total = jnp.zeros((TOKENS, D), jnp.float32)
    for shard_index in range(N_TENSOR):
        grad_cols = out_grad[:, shard_index * width_dev:(shard_index + 1) * width_dev]
        weight_cols = base_weight[:, shard_index * width_dev:(shard_index + 1) * width_dev]
        base_back = lax.dot_general(grad_cols, weight_cols, (((1,), (1,)), ((), ())), preferred_element_type=jnp.float32)

        def add_back(slot_index, running):

            def update(state):
                grad_slab = lax.dynamic_slice_in_dim(out_grad, slot_head[slot_index] * HEAD_DIM, HEAD_DIM, 1)
                delta_term = lax.dot_general(grad_slab, blocks[slot_index], (((1,), (1,)), ((), ())), preferred_element_type=jnp.float32)
                row_start = slot_row[slot_index] * HEAD_DIM
                current = lax.dynamic_slice_in_dim(state, row_start, HEAD_DIM, 1)
                return lax.dynamic_update_slice_in_dim(state, current + delta_term, row_start, 1)
            owned = jnp.logical_and(slot_live[slot_index] > 0, slot_head[slot_index] // heads_dev == shard_index)
            return lax.cond(owned, update, lambda state: state, running)
        base_back = lax.fori_loop(0, SLOTS, add_back, base_back)
        rounded = lax.optimization_barrier(base_back.astype(jnp.bfloat16))
        total = total + rounded.astype(jnp.float32)
    input_grad = total.astype(jnp.bfloat16)
    grad_scale = 1.0 / math.sqrt(TOKENS)

    def grad_one(slot_index):
        token_slab = lax.dynamic_slice_in_dim(tokens, slot_row[slot_index] * HEAD_DIM, HEAD_DIM, 1)
        grad_slab = lax.dynamic_slice_in_dim(out_grad, slot_head[slot_index] * HEAD_DIM, HEAD_DIM, 1)
        grad_block = lax.dot_general(token_slab, grad_slab, (((0,), (0,)), ((), ())), preferred_element_type=jnp.float32)
        weight_live = slot_live[slot_index].astype(jnp.float32) * grad_scale
        return (grad_block * weight_live).reshape(HEAD_DIM * HEAD_DIM)
    block_grad = lax.map(grad_one, jnp.arange(SLOTS, dtype=jnp.int32))
    first_new = 0.9 * moment1 + 0.1 * block_grad
    second_new = 0.999 * moment2 + 0.001 * block_grad * block_grad
    update_step = 0.02 * (first_new / CORRECT_ONE) / (jnp.sqrt(second_new / CORRECT_TWO) + 1e-08)
    new_delta = (delta.astype(jnp.float32) - update_step).astype(jnp.bfloat16)
    return (projected, input_grad, new_delta, first_new, second_new)
```

```python
import functools
import math

import jax
import jax.numpy as jnp
from jax import lax
from jax.experimental import pallas as pl
from jax.experimental.pallas import tpu as pltpu
from jax.sharding import PartitionSpec as P

HEAD_DIM = 128
LANES = 128
CORRECT_ONE = 1.0 - 0.9**10
CORRECT_TWO = 1.0 - 0.999**10
BF16 = jnp.bfloat16
F32 = jnp.float32
VMEM_LIMIT = 48 * 1024 * 1024
BACK_CHUNKS = 2
TILE = 512


def params():
    return pltpu.CompilerParams(vmem_limit_bytes=VMEM_LIMIT)


def vmem(n=1):
    return [pl.BlockSpec(memory_space=pltpu.VMEM)] * n


def smem(n=1):
    return [pl.BlockSpec(memory_space=pltpu.SMEM)] * n


def bits_of(count):
    return [1 << i for i in range(count.bit_length() - 1)]


def halving_order(count):
    order = [0]
    for bit in reversed(bits_of(count)):
        order = order + [j + bit for j in order]
    width = count.bit_length() - 1
    rev = lambda j: int(format(j, "0%db" % width)[::-1], 2) if width else 0
    return sorted(range(count), key=rev)


def xor_permute(x, axis, bit):
    count = lax.axis_size(axis)
    return lax.ppermute(x, axis, [(i, i ^ bit) for i in range(count)])


def slot_ranks(owner_ref, nb):
    ranks = []
    for b in range(nb):
        rank = jnp.int32(0)
        for before in range(b):
            rank = rank + (owner_ref[before] == owner_ref[b]).astype(jnp.int32)
        ranks.append(rank)
    return ranks


def lane_block(index):
    return pl.ds(pl.multiple_of(index * LANES, LANES), LANES)


def row_block(index, rows):
    return pl.ds(pl.multiple_of(index * rows, rows), rows)


def pick_kernel(nt, nb, index_ref, grad_ref, perm_ref, *piece_refs):
    me = lax.axis_index("tensor")
    rows = grad_ref.shape[0] // nt
    heads = grad_ref.shape[1] // HEAD_DIM
    for p, j in enumerate(halving_order(nt)):
        perm_ref[p * rows : (p + 1) * rows, :] = grad_ref[row_block(me ^ j, rows), :]
    for b in range(nb):
        head = index_ref[b, 1]
        mine = head // heads == me
        local = jnp.where(mine, head - me * heads, 0)
        cols = slice(b * LANES, (b + 1) * LANES)
        for j in range(nt):
            part = grad_ref[row_block(me ^ j, rows), lane_block(local)]
            piece_refs[j][:, cols] = jnp.where(mine, part, jnp.zeros_like(part))


def picks(block_index, out_grad, nt):
    nb = block_index.shape[0]
    rows = out_grad.shape[0] // nt
    return pl.pallas_call(
        functools.partial(pick_kernel, nt, nb),
        out_shape=[jax.ShapeDtypeStruct(out_grad.shape, BF16)]
        + [jax.ShapeDtypeStruct((rows, nb * LANES), BF16)] * nt,
        in_specs=smem() + vmem(),
        out_specs=vmem(1 + nt),
        compiler_params=params(),
        name="picks",
    )(block_index, out_grad)


def grad_kernel(nt, nd, nb, cap, scale, index_ref, owner_ref, tok_ref, *refs):
    piece_refs = refs[:nt]
    picked_ref, keep_ref, send_ref, block_ref = refs[nt:]
    me = lax.axis_index("tensor")
    dp = lax.axis_index("dp")
    part = HEAD_DIM // nt
    total = piece_refs[0][...].astype(F32)
    for j in range(1, nt):
        total = total + piece_refs[j][...].astype(F32)
    picked_ref[...] = total.astype(BF16)
    keep_ref[...] = jnp.zeros_like(keep_ref)
    send_ref[...] = jnp.zeros_like(send_ref)
    ranks = slot_ranks(owner_ref, nb)
    width = nd.bit_length() - 1
    order = halving_order(nt)
    half = nt // 2
    for b in range(nb):
        slab = tok_ref[:, lane_block(index_ref[b, 0])]
        block_ref[b] = (
            lax.dot_general(
                slab,
                picked_ref[:, b * LANES : (b + 1) * LANES],
                (((0,), (0,)), ((), ())),
                preferred_element_type=F32,
            )
            * scale
        ).astype(BF16)
        away = owner_ref[b] ^ dp
        place = jnp.int32(0)
        for i in range(width):
            place = place + ((away >> i) & 1) * (1 << (width - 1 - i))
        for p, j in enumerate(order):
            target = keep_ref if p < half else send_ref
            start = ((place * half + p % half) * cap + ranks[b]) * part
            target[pl.ds(pl.multiple_of(start, part), part), :] = block_ref[b, row_block(me ^ j, part), :]


def block_grads(block_index, block_owner, tokens, pieces, nt, nd, cap):
    nb = block_index.shape[0]
    rows = tokens.shape[0]
    scale = 1.0 / math.sqrt(rows * nt * nd)
    size = nd * (nt // 2) * cap * (HEAD_DIM // nt)
    return pl.pallas_call(
        functools.partial(grad_kernel, nt, nd, nb, cap, scale),
        out_shape=[
            jax.ShapeDtypeStruct((rows, nb * LANES), BF16),
            jax.ShapeDtypeStruct((size, LANES), BF16),
            jax.ShapeDtypeStruct((size, LANES), BF16),
        ],
        in_specs=smem(2) + vmem(1 + nt),
        out_specs=vmem(3),
        scratch_shapes=[pltpu.VMEM((nb, HEAD_DIM, HEAD_DIM), BF16)],
        compiler_params=params(),
        name="block_grads",
    )(block_index, block_owner, tokens, *pieces)


def first_step_kernel(cap, keep_ref, recv_ref, delta_ref, keep_out, send_out):
    half = keep_out.shape[0]
    part = delta_ref.shape[1] // LANES
    total = (keep_ref[...].astype(F32) + recv_ref[...].astype(F32)).astype(BF16)
    keep_out[...] = total[:half]
    send_out[:half, :] = total[half:]
    delta = delta_ref[...].astype(F32)
    for k in range(cap):
        lines = [delta[k : k + 1, i * LANES : (i + 1) * LANES] for i in range(part)]
        send_out[half + k * part : half + (k + 1) * part, :] = jnp.concatenate(lines, 0).astype(BF16)


def first_step(keep, recv, delta):
    cap = delta.shape[0]
    rows = keep.shape[0]
    extra = cap * delta.shape[1] // LANES
    return pl.pallas_call(
        functools.partial(first_step_kernel, cap),
        out_shape=[
            jax.ShapeDtypeStruct((rows // 2, LANES), BF16),
            jax.ShapeDtypeStruct((rows // 2 + extra, LANES), BF16),
        ],
        in_specs=vmem(3),
        out_specs=vmem(2),
        compiler_params=params(),
        name="first_step",
    )(keep, recv, delta)


def step_kernel(keep_ref, sent_ref, recv_ref, keep_out, send_out):
    rows = keep_ref.shape[0]
    half = rows // 2
    extra = sent_ref.shape[0] - rows
    total = (keep_ref[...].astype(F32) + recv_ref[:rows, :].astype(F32)).astype(BF16)
    keep_out[...] = total[:half]
    send_out[:half, :] = total[half:]
    send_out[half : half + extra, :] = sent_ref[rows:, :]
    send_out[half + extra :, :] = recv_ref[rows:, :]


def step(keep, sent, recv):
    rows = keep.shape[0]
    extra = sent.shape[0] - rows
    return pl.pallas_call(
        step_kernel,
        out_shape=[
            jax.ShapeDtypeStruct((rows // 2, LANES), BF16),
            jax.ShapeDtypeStruct((rows // 2 + 2 * extra, LANES), BF16),
        ],
        in_specs=vmem(3),
        out_specs=vmem(2),
        compiler_params=params(),
        name="chain_step",
    )(keep, sent, recv)


def compact_kernel(nb, cap, part, owner_ref, keep_ref, sent_ref, recv_ref, keep_out, send_out, all_ref):
    dp = lax.axis_index("dp")
    rows = keep_ref.shape[0]
    half = rows // 2
    extra = sent_ref.shape[0] - rows
    total = (keep_ref[...].astype(F32) + recv_ref[:rows, :].astype(F32)).astype(BF16)
    keep_out[...] = total[:half]
    send_out[:half, :] = total[half:]
    all_ref[:extra, :] = sent_ref[rows:, :]
    all_ref[extra:, :] = recv_ref[rows:, :]
    ranks = slot_ranks(owner_ref, nb)
    for b in range(nb):
        place = (owner_ref[b] ^ dp) * cap + ranks[b]
        send_out[half + b * part : half + (b + 1) * part, :] = all_ref[row_block(place, part), :]


def compact(block_owner, keep, sent, recv, cap, part):
    nb = block_owner.shape[0]
    rows = keep.shape[0]
    extra = sent.shape[0] - rows
    return pl.pallas_call(
        functools.partial(compact_kernel, nb, cap, part),
        out_shape=[
            jax.ShapeDtypeStruct((rows // 2, LANES), BF16),
            jax.ShapeDtypeStruct((rows // 2 + nb * part, LANES), BF16),
        ],
        in_specs=smem() + vmem(3),
        out_specs=vmem(2),
        scratch_shapes=[pltpu.VMEM((2 * extra, LANES), BF16)],
        compiler_params=params(),
        name="compact_step",
    )(block_owner, keep, sent, recv)


def adam_kernel(
    cap, keep_ref, sent_ref, recv_ref, delta_ref, one_ref, two_ref,
    blocks_out, delta_out, one_out, two_out, grad_ref,
):
    rows = keep_ref.shape[0]
    part = rows // cap
    extra = sent_ref.shape[0] - rows
    blocks_out[:extra, :] = sent_ref[rows:, :]
    blocks_out[extra:, :] = recv_ref[rows:, :]
    total = keep_ref[...].astype(F32) + recv_ref[:rows, :].astype(F32)
    for k in range(cap):
        for i in range(part):
            grad_ref[k : k + 1, i * LANES : (i + 1) * LANES] = total[k * part + i : k * part + i + 1, :]
    grad = grad_ref[...]
    first = 0.9 * one_ref[...] + 0.1 * grad
    second = 0.999 * two_ref[...] + 0.001 * grad * grad
    one_out[...] = first
    two_out[...] = second
    update = 0.02 * (first / CORRECT_ONE) / (jnp.sqrt(second / CORRECT_TWO) + 1e-08)
    delta_out[...] = (delta_ref[...].astype(F32) - update).astype(BF16)


def adam(keep, sent, recv, delta, moment1, moment2):
    rows = keep.shape[0]
    extra = sent.shape[0] - rows
    return pl.pallas_call(
        functools.partial(adam_kernel, delta.shape[0]),
        out_shape=[
            jax.ShapeDtypeStruct((2 * extra, LANES), BF16),
            jax.ShapeDtypeStruct(delta.shape, BF16),
            jax.ShapeDtypeStruct(delta.shape, F32),
            jax.ShapeDtypeStruct(delta.shape, F32),
        ],
        in_specs=vmem(6),
        out_specs=vmem(4),
        scratch_shapes=[pltpu.VMEM(delta.shape, F32)],
        compiler_params=params(),
        name="adam",
    )(keep, sent, recv, delta, moment1, moment2)


def back_kernel(grad_ref, weight_ref, keep_ref, send_ref):
    half = keep_ref.shape[0]
    out = lax.dot_general(
        grad_ref[...], weight_ref[...], (((1,), (1,)), ((), ())), preferred_element_type=F32
    ).astype(BF16)
    keep_ref[...] = out[:half]
    send_ref[...] = out[half:]


def back(grad, weight, chunk):
    rows = grad.shape[0]
    depth, cols = weight.shape
    width = depth // BACK_CHUNKS
    steps = width // TILE
    half = jax.ShapeDtypeStruct((rows // 2, width), BF16)
    return pl.pallas_call(
        back_kernel,
        grid=(steps,),
        out_shape=[half, half],
        in_specs=[
            pl.BlockSpec((rows, cols), lambda i: (0, 0)),
            pl.BlockSpec((TILE, cols), lambda i: (chunk * steps + i, 0)),
        ],
        out_specs=[pl.BlockSpec((rows // 2, TILE), lambda i: (0, i))] * 2,
        compiler_params=params(),
        cost_estimate=pl.CostEstimate(
            flops=2 * rows * width * cols, bytes_accessed=2 * width * cols + 2 * rows * width, transcendentals=0
        ),
        name="back",
    )(grad, weight)


def merge_kernel(keep_ref, recv_ref, keep_out, send_out):
    half = keep_out.shape[0]
    total = (keep_ref[...].astype(F32) + recv_ref[...].astype(F32)).astype(BF16)
    keep_out[...] = total[:half]
    send_out[...] = total[half:]


def merge(keep, recv):
    half = jax.ShapeDtypeStruct((keep.shape[0] // 2, keep.shape[1]), BF16)
    return pl.pallas_call(
        merge_kernel,
        out_shape=[half, half],
        in_specs=vmem(2),
        out_specs=vmem(2),
        compiler_params=params(),
        name="merge",
    )(keep, recv)


def load_block(block_ref, halves, order, b, nb, part, me):
    per = len(order) // 2
    for p, j in enumerate(order):
        source = halves[p // per]
        start = ((p % per) * nb + b) * part
        block_ref[row_block(me ^ j, part), :] = source[start : start + part, :]


def gather_order(nt):
    order = [0]
    for bit in bits_of(nt)[1:] + [1]:
        order = order + [j ^ bit for j in order]
    return order


def forward_kernel(nt, nb, steps, index_ref, *refs):
    token_refs = refs[:nt]
    near_ref, far_ref, weight_ref, out_ref, acc_ref, block_ref = refs[nt:]
    me = lax.axis_index("tensor")
    i = pl.program_id(0)
    order = gather_order(nt)
    rows = token_refs[0].shape[0]
    heads = out_ref.shape[1] // HEAD_DIM
    part = HEAD_DIM // nt

    def slab(cols):
        return jnp.concatenate([ref[:, cols] for ref in token_refs], axis=0)

    tile = slab(pl.ds(pl.multiple_of(i * TILE, TILE), TILE))
    product = jnp.dot(tile, weight_ref[...], preferred_element_type=F32)

    @pl.when(i == 0)
    def _():
        acc_ref[...] = product

    @pl.when(i > 0)
    def _():
        acc_ref[...] += product

    @pl.when(i == steps - 1)
    def _():
        for b in range(nb):
            head = index_ref[b, 1]

            @pl.when(head // heads == me)
            def _():
                load_block(block_ref, (near_ref, far_ref), order, b, nb, part, me)
                cols = lane_block(head - me * heads)
                acc_ref[:, cols] += jnp.dot(
                    slab(lane_block(index_ref[b, 0])), block_ref[...], preferred_element_type=F32
                )

        for p, j in enumerate(order):
            out_ref[row_block(me ^ j, rows), :] = acc_ref[p * rows : (p + 1) * rows, :].astype(BF16)


def forward(block_index, pieces, near, far, weight, nt):
    nb = block_index.shape[0]
    rows = pieces[0].shape[0] * nt
    depth, cols = weight.shape
    steps = depth // TILE
    whole = lambda x: pl.BlockSpec(x.shape, lambda i: (0, 0))
    return pl.pallas_call(
        functools.partial(forward_kernel, nt, nb, steps),
        grid=(steps,),
        out_shape=jax.ShapeDtypeStruct((rows, cols), BF16),
        in_specs=smem()
        + [whole(x) for x in pieces]
        + [whole(near), whole(far)]
        + [pl.BlockSpec((TILE, cols), lambda i: (i, 0))],
        out_specs=pl.BlockSpec((rows, cols), lambda i: (0, 0)),
        scratch_shapes=[pltpu.VMEM((rows, cols), F32), pltpu.VMEM((HEAD_DIM, HEAD_DIM), BF16)],
        compiler_params=params(),
        cost_estimate=pl.CostEstimate(
            flops=2 * rows * depth * cols, bytes_accessed=2 * depth * cols + 2 * rows * depth, transcendentals=0
        ),
        name="forward",
    )(block_index, *pieces, near, far, weight)


def final_kernel(nt, nb, chunks, index_ref, picked_ref, near_ref, far_ref, *refs):
    keeps, recvs = refs[:chunks], refs[chunks : 2 * chunks]
    out_ref, sum_ref, block_ref = refs[2 * chunks :]
    me = lax.axis_index("tensor")
    order = gather_order(nt)
    part = HEAD_DIM // nt
    width = keeps[0].shape[1]
    for c in range(chunks):
        sum_ref[:, c * width : (c + 1) * width] = keeps[c][...].astype(F32) + recvs[c][...].astype(F32)
    for b in range(nb):
        load_block(block_ref.at[b], (near_ref, far_ref), order, b, nb, part, me)
        sum_ref[:, lane_block(index_ref[b, 0])] += lax.dot_general(
            picked_ref[:, b * LANES : (b + 1) * LANES],
            block_ref[b],
            (((1,), (1,)), ((), ())),
            preferred_element_type=F32,
        )
    out_ref[...] = sum_ref[...].astype(BF16)


def final(block_index, picked, near, far, keeps, recvs, nt):
    nb = block_index.shape[0]
    chunks = len(keeps)
    rows, width = keeps[0].shape
    return pl.pallas_call(
        functools.partial(final_kernel, nt, nb, chunks),
        out_shape=jax.ShapeDtypeStruct((rows, width * chunks), BF16),
        in_specs=smem() + vmem(3 + 2 * chunks),
        out_specs=pl.BlockSpec(memory_space=pltpu.VMEM),
        scratch_shapes=[
            pltpu.VMEM((rows, width * chunks), F32),
            pltpu.VMEM((nb, HEAD_DIM, HEAD_DIM), BF16),
        ],
        compiler_params=params(),
        name="final",
    )(block_index, picked, near, far, *keeps, *recvs)


def on_device(tokens, base_weight, out_grad, block_index, block_owner, delta, moment1, moment2):
    nt = lax.axis_size("tensor")
    nd = lax.axis_size("dp")
    cap = delta.shape[0]
    part = HEAD_DIM // nt
    outer = bits_of(nt)[1:]

    gathered = [tokens]
    for bit in outer:
        gathered = gathered + [xor_permute(x, "tensor", bit) for x in gathered]
    gathered = gathered + [xor_permute(x, "tensor", 1) for x in gathered]

    perm, *pieces = picks(block_index, out_grad, nt)
    pieces = [pieces[0]] + [xor_permute(pieces[j], "tensor", j) for j in range(1, nt)]

    picked, keep, send = block_grads(block_index, block_owner, tokens, pieces, nt, nd, cap)
    recv = xor_permute(send, "tensor", 1)
    keep, send = first_step(keep, recv, delta)
    dp_bits = bits_of(nd)
    for bit in dp_bits[:-1]:
        recv = xor_permute(send, "dp", bit)
        keep, send = step(keep, send, recv)
    recv = xor_permute(send, "dp", dp_bits[-1])
    keep, send = compact(block_owner, keep, send, recv, cap, part)
    for bit in outer[:-1]:
        recv = xor_permute(send, "tensor", bit)
        keep, send = step(keep, send, recv)
    recv = xor_permute(send, "tensor", outer[-1])
    near, new_delta, first_new, second_new = adam(keep, send, recv, delta, moment1, moment2)
    far = xor_permute(near, "tensor", 1)

    keeps, recvs = [], []
    for chunk in range(BACK_CHUNKS):
        keep, send = back(perm, base_weight, chunk)
        for bit in bits_of(nt)[:-1]:
            keep, send = merge(keep, xor_permute(send, "tensor", bit))
        keeps.append(keep)
        recvs.append(xor_permute(send, "tensor", bits_of(nt)[-1]))

    projected = forward(block_index, gathered, near, far, base_weight, nt)
    input_grad = final(block_index, picked, near, far, keeps, recvs, nt)
    return (projected, input_grad, new_delta, first_new, second_new)


def solution(mesh):
    placed = (
        P(("dp", "tensor"), None),
        P(None, "tensor"),
        P("dp", "tensor"),
        P(),
        P(),
        P("dp", "tensor"),
        P("dp", "tensor"),
        P("dp", "tensor"),
    )
    return jax.shard_map(
        on_device,
        mesh=mesh,
        in_specs=placed,
        out_specs=(
            P("dp", "tensor"),
            P(("dp", "tensor"), None),
            P("dp", "tensor"),
            P("dp", "tensor"),
            P("dp", "tensor"),
        ),
        check_vma=False,
    )
```

```python
import functools
import math

import jax
import jax.numpy as jnp
from jax import lax
from jax.experimental import pallas as pl
from jax.experimental.pallas import tpu as pltpu
from jax.sharding import PartitionSpec as P

HEAD_DIM = 128
LANES = 128
CORRECT_ONE = 1.0 - 0.9**10
CORRECT_TWO = 1.0 - 0.999**10
BF16 = jnp.bfloat16
F32 = jnp.float32
VMEM_LIMIT = 24 * 1024 * 1024
BACK_PIECES = 4
BACK_CHUNKS = 2
ORDER = (
    ("grad", 0), ("back", 0), ("grad", 1), ("back", 1), ("sum", 0), ("back", 2), ("grad", 2), ("relay", 0), ("back", 3), ("sum", 1), ("forward", 0), ("grad", 3), ("grad", 4), ("project", 0), ("correct", 0), ("adam", 0), ("final", 0),
)


def params():
    return pltpu.CompilerParams(vmem_limit_bytes=VMEM_LIMIT)


def cost(us):
    return pl.CostEstimate(flops=int(us * 1e9), bytes_accessed=int(us * 1e6), transcendentals=0)


def vmem(n=1):
    return [pl.BlockSpec(memory_space=pltpu.VMEM)] * n


def anywhere(deps):
    return [pl.BlockSpec(memory_space=pl.ANY)] * len(deps)


def with_deps(kernel, inputs, deps):
    def run(*refs):
        kernel(*refs[:inputs], *refs[inputs + len(deps) :])

    return run


def bits_of(count):
    return [1 << i for i in range(count.bit_length() - 1)]


def halving_order(count):
    order = [0]
    for bit in reversed(bits_of(count)):
        order = order + [j + bit for j in order]
    width = count.bit_length() - 1
    rev = lambda j: int(format(j, "0%db" % width)[::-1], 2) if width else 0
    return sorted(range(count), key=rev)


def gather_order(nt):
    order = [0]
    for bit in bits_of(nt)[1:] + [1]:
        order = order + [j ^ bit for j in order]
    return order


def xor_permute(x, axis, bit):
    count = lax.axis_size(axis)
    return lax.ppermute(x, axis, [(i, i ^ bit) for i in range(count)])


def slot_ranks(owners):
    ranks = []
    for b, owner in enumerate(owners):
        rank = jnp.int32(0)
        for before in owners[:b]:
            rank = rank + (before == owner).astype(jnp.int32)
        ranks.append(rank)
    return ranks


def scalars(ref, row, nb):
    table = ref[...]
    return [table[row, b] for b in range(nb)]


def place_of(offset, bits):
    place = jnp.int32(0)
    for i, bit in enumerate(bits):
        place = place + jnp.where((offset & bit) != 0, 1 << i, 0)
    return place


def lane_block(index):
    return pl.ds(pl.multiple_of(index * LANES, LANES), LANES)


def row_block(index, rows):
    return pl.ds(pl.multiple_of(index * rows, rows), rows)


def relay_kernel(count, *refs):
    for i in range(count):
        refs[count + i][...] = refs[i][...]


def relay(parts, deps):
    count = len(parts)
    return list(
        pl.pallas_call(
            with_deps(functools.partial(relay_kernel, count), count, deps),
            out_shape=[jax.ShapeDtypeStruct(x.shape, x.dtype) for x in parts],
            in_specs=vmem(count) + anywhere(deps),
            out_specs=vmem(count),
            compiler_params=params(),
            cost_estimate=cost(0.01),
            name="relay",
        )(*parts, *deps)
    )


def begin_kernel(out_ref):
    out_ref[...] = jnp.zeros_like(out_ref)


def begin():
    return pl.pallas_call(
        begin_kernel,
        out_shape=jax.ShapeDtypeStruct((8, LANES), F32),
        out_specs=pl.BlockSpec(memory_space=pltpu.VMEM),
        compiler_params=params(),
        cost_estimate=cost(30),
        name="begin",
    )()


def slab_kernel(nb, index_ref, tok_ref, delta_ref, out_ref):
    rows = tok_ref.shape[0]
    cap = delta_ref.shape[0]
    part = delta_ref.shape[1] // LANES
    delta = delta_ref[...].astype(F32)
    for k in range(cap):
        lines = [delta[k : k + 1, i * LANES : (i + 1) * LANES] for i in range(part)]
        start = nb * rows + k * part
        out_ref[start : start + part, :] = jnp.concatenate(lines, 0).astype(BF16)
    row_of = scalars(index_ref, 0, nb)
    for b in range(nb):
        out_ref[b * rows : (b + 1) * rows, :] = tok_ref[:, lane_block(row_of[b])]


def slabs(index, tokens, delta, deps):
    nb = index.shape[1]
    return pl.pallas_call(
        with_deps(functools.partial(slab_kernel, nb), 3, deps),
        out_shape=jax.ShapeDtypeStruct((nb * tokens.shape[0] + delta.size // LANES, LANES), BF16),
        in_specs=vmem(3) + anywhere(deps),
        out_specs=pl.BlockSpec(memory_space=pltpu.VMEM),
        compiler_params=params(),
        cost_estimate=cost(30),
        name="slabs",
    )(index, tokens, delta, *deps)


def spread_kernel(size, own_ref, recv_ref, slab_out, line_out):
    slab_out[:size, :] = own_ref[:size, :]
    slab_out[size : 2 * size, :] = recv_ref[:size, :]
    extra = own_ref.shape[0] - size
    line_out[:extra, :] = own_ref[size:, :]
    line_out[extra : 2 * extra, :] = recv_ref[size:, :]


def spread(own, recv, size, deps):
    extra = own.shape[0] - size
    return pl.pallas_call(
        with_deps(functools.partial(spread_kernel, size), 2, deps),
        out_shape=[
            jax.ShapeDtypeStruct((2 * size, LANES), BF16),
            jax.ShapeDtypeStruct((2 * extra, LANES), BF16),
        ],
        in_specs=vmem(2) + anywhere(deps),
        out_specs=vmem(2),
        compiler_params=params(),
        cost_estimate=cost(20),
        name="spread",
    )(own, recv, *deps)


def grad_kernel(
    nt, bits, nb, cap, scale, index_ref, owner_ref, near_ref, far_ref, grad_ref, keep_ref, send_ref, slab_ref, block_ref
):
    me = lax.axis_index("tensor")
    dp = lax.axis_index("dp")
    part = HEAD_DIM // nt
    rows = grad_ref.shape[0] // nt
    heads = grad_ref.shape[1] // HEAD_DIM
    half = nt // 2
    keep_ref[...] = jnp.zeros_like(keep_ref)
    send_ref[...] = jnp.zeros_like(send_ref)
    owners = scalars(owner_ref, 0, nb)
    ranks = slot_ranks(owners)
    head_of = scalars(index_ref, 1, nb)
    for b in range(nb):
        head = head_of[b]

        @pl.when(head // heads == me)
        def _():
            for p, j in enumerate(gather_order(nt)):
                source = near_ref if p < half else far_ref
                start = ((p % half) * nb + b) * rows
                slab_ref[row_block(me ^ j, rows), :] = source[start : start + rows, :]
            block_ref[...] = (
                lax.dot_general(
                    slab_ref[...],
                    grad_ref[:, lane_block(head - me * heads)],
                    (((0,), (0,)), ((), ())),
                    preferred_element_type=F32,
                )
                * scale
            ).astype(BF16)
            place = place_of(owners[b] ^ dp, bits[::-1])
            for p, j in enumerate(halving_order(nt)):
                target = keep_ref if p < half else send_ref
                start = ((place * half + p % half) * cap + ranks[b]) * part
                target[pl.ds(pl.multiple_of(start, part), part), :] = block_ref[row_block(me ^ j, part), :]


def block_grads(index, owner, near, far, out_grad, nt, bits, cap, deps):
    nb = index.shape[1]
    rows = out_grad.shape[0]
    nd = 1 << len(bits)
    scale = 1.0 / math.sqrt(rows * nd)
    size = nd * (nt // 2) * cap * (HEAD_DIM // nt)
    half = jax.ShapeDtypeStruct((size, LANES), BF16)
    return pl.pallas_call(
        with_deps(functools.partial(grad_kernel, nt, bits, nb, cap, scale), 5, deps),
        out_shape=[half, half],
        in_specs=vmem(5) + anywhere(deps),
        out_specs=vmem(2),
        scratch_shapes=[pltpu.VMEM((rows, LANES), BF16), pltpu.VMEM((HEAD_DIM, HEAD_DIM), BF16)],
        compiler_params=params(),
        cost_estimate=cost(0.01),
        name="block_grads",
    )(index, owner, near, far, out_grad, *deps)


def halve_kernel(keep_ref, recv_ref, keep_out, send_out):
    half = keep_out.shape[0]
    total = (keep_ref[...].astype(F32) + recv_ref[...].astype(F32)).astype(BF16)
    keep_out[...] = total[:half]
    send_out[...] = total[half:]


def halve(keep, recv, deps):
    rows = keep.shape[0]
    half = jax.ShapeDtypeStruct((rows // 2, LANES), BF16)
    return pl.pallas_call(
        with_deps(halve_kernel, 2, deps),
        out_shape=[half, half],
        in_specs=vmem(2) + anywhere(deps),
        out_specs=vmem(2),
        compiler_params=params(),
        cost_estimate=cost(0.01),
        name="halve",
    )(keep, recv, *deps)


def first_kernel(keep_ref, recv_ref, lines_ref, keep_out, send_out):
    half = keep_out.shape[0]
    total = (keep_ref[...].astype(F32) + recv_ref[...].astype(F32)).astype(BF16)
    keep_out[...] = total[:half]
    send_out[:half, :] = total[half:]
    send_out[half:, :] = lines_ref[...]


def first_step(keep, recv, lines, deps):
    half = keep.shape[0] // 2
    return pl.pallas_call(
        with_deps(first_kernel, 3, deps),
        out_shape=[
            jax.ShapeDtypeStruct((half, LANES), BF16),
            jax.ShapeDtypeStruct((half + lines.shape[0], LANES), BF16),
        ],
        in_specs=vmem(3) + anywhere(deps),
        out_specs=vmem(2),
        compiler_params=params(),
        cost_estimate=cost(0.01),
        name="first_step",
    )(keep, recv, lines, *deps)


def step_kernel(keep_ref, sent_ref, recv_ref, keep_out, send_out):
    rows = keep_ref.shape[0]
    half = rows // 2
    extra = sent_ref.shape[0] - rows
    total = (keep_ref[...].astype(F32) + recv_ref[:rows, :].astype(F32)).astype(BF16)
    keep_out[...] = total[:half]
    send_out[:half, :] = total[half:]
    send_out[half : half + extra, :] = sent_ref[rows:, :]
    send_out[half + extra :, :] = recv_ref[rows:, :]


def step(keep, sent, recv, deps):
    rows = keep.shape[0]
    extra = sent.shape[0] - rows
    return pl.pallas_call(
        with_deps(step_kernel, 3, deps),
        out_shape=[
            jax.ShapeDtypeStruct((rows // 2, LANES), BF16),
            jax.ShapeDtypeStruct((rows // 2 + 2 * extra, LANES), BF16),
        ],
        in_specs=vmem(3) + anywhere(deps),
        out_specs=vmem(2),
        compiler_params=params(),
        cost_estimate=cost(0.01),
        name="chain_step",
    )(keep, sent, recv, *deps)


def compact_kernel(bits, nb, cap, part, tensor, owner_ref, keep_ref, sent_ref, recv_ref, keep_out, send_out, out_ref, all_ref):
    dp = lax.axis_index("dp")
    rows = keep_ref.shape[0]
    half = rows // 2
    extra = sent_ref.shape[0] - rows
    total = (keep_ref[...].astype(F32) + recv_ref[:rows, :].astype(F32)).astype(BF16)
    keep_out[...] = total[:half]
    send_out[...] = total[half:]
    all_ref[:extra, :] = sent_ref[rows:, :]
    all_ref[extra:, :] = recv_ref[rows:, :]
    owners = scalars(owner_ref, 0, nb)
    ranks = slot_ranks(owners)
    for b in range(nb):
        place = place_of(owners[b] ^ dp, bits)
        for t in range(tensor):
            start = ((place * tensor + t) * cap + ranks[b]) * part
            out_ref[(t * nb + b) * part : (t * nb + b + 1) * part, :] = all_ref[
                pl.ds(pl.multiple_of(start, part), part), :
            ]


def compact(owner, keep, sent, recv, bits, cap, part, tensor, deps):
    nb = owner.shape[1]
    rows = keep.shape[0]
    half = jax.ShapeDtypeStruct((rows // 2, LANES), BF16)
    return pl.pallas_call(
        with_deps(functools.partial(compact_kernel, bits, nb, cap, part, tensor), 4, deps),
        out_shape=[half, half, jax.ShapeDtypeStruct((tensor * nb * part, LANES), BF16)],
        in_specs=vmem(4) + anywhere(deps),
        out_specs=vmem(3),
        scratch_shapes=[pltpu.VMEM((2 * (sent.shape[0] - rows), LANES), BF16)],
        compiler_params=params(),
        cost_estimate=cost(0.01),
        name="compact_step",
    )(owner, keep, sent, recv, *deps)


def adam_kernel(
    cap, keep_ref, recv_ref, delta_ref, one_ref, two_ref, delta_out, one_out, two_out, grad_ref
):
    part = keep_ref.shape[0] // cap
    total = keep_ref[...].astype(F32) + recv_ref[...].astype(F32)
    for k in range(cap):
        for i in range(part):
            grad_ref[k : k + 1, i * LANES : (i + 1) * LANES] = total[k * part + i : k * part + i + 1, :]
    grad = grad_ref[...]
    first = 0.9 * one_ref[...] + 0.1 * grad
    second = 0.999 * two_ref[...] + 0.001 * grad * grad
    one_out[...] = first
    two_out[...] = second
    update = 0.02 * (first / CORRECT_ONE) / (jnp.sqrt(second / CORRECT_TWO) + 1e-08)
    delta_out[...] = (delta_ref[...].astype(F32) - update).astype(BF16)


def adam(keep, recv, delta, moment1, moment2, deps):
    return pl.pallas_call(
        with_deps(functools.partial(adam_kernel, delta.shape[0]), 5, deps),
        out_shape=[
            jax.ShapeDtypeStruct(delta.shape, BF16),
            jax.ShapeDtypeStruct(delta.shape, F32),
            jax.ShapeDtypeStruct(delta.shape, F32),
        ],
        in_specs=vmem(5) + anywhere(deps),
        out_specs=vmem(3),
        scratch_shapes=[pltpu.VMEM(delta.shape, F32)],
        compiler_params=params(),
        cost_estimate=cost(0.01),
        name="adam",
    )(keep, recv, delta, moment1, moment2, *deps)


def back_kernel(nt, nb, start, width, index_ref, grad_ref, weight_ref, keep_ref, send_ref, perm_ref):
    me = lax.axis_index("tensor")
    rows = grad_ref.shape[0] // nt
    heads = grad_ref.shape[1] // HEAD_DIM
    half = nt // 2 * rows
    for p, j in enumerate(halving_order(nt)):
        perm_ref[p * rows : (p + 1) * rows, :] = grad_ref[row_block(me ^ j, rows), :]
    out = lax.dot_general(
        weight_ref[start : start + width, :], perm_ref[...], (((1,), (1,)), ((), ())), preferred_element_type=F32
    )
    out = out.astype(BF16).T
    keep_ref[:, :width] = out[:half]
    send_ref[:, :width] = out[half:]
    if keep_ref.shape[1] > width:
        head_of = scalars(index_ref, 1, nb)
        for b in range(nb):
            head = head_of[b]
            mine = head // heads == me
            part = perm_ref[:, lane_block(jnp.where(mine, head - me * heads, 0))]
            part = jnp.where(mine, part, jnp.zeros_like(part))
            cols = slice(width + b * LANES, width + (b + 1) * LANES)
            keep_ref[:, cols] = part[:half]
            send_ref[:, cols] = part[half:]


def back(index, out_grad, weight, piece, riders, nt, deps):
    nb = index.shape[1]
    rows = out_grad.shape[0]
    depth = weight.shape[0]
    width = depth // BACK_PIECES
    half = jax.ShapeDtypeStruct((rows // 2, width + (nb * LANES if riders else 0)), BF16)
    return pl.pallas_call(
        with_deps(functools.partial(back_kernel, nt, nb, piece * width, width), 3, deps),
        out_shape=[half, half],
        in_specs=vmem(3) + anywhere(deps),
        out_specs=vmem(2),
        scratch_shapes=[pltpu.VMEM(out_grad.shape, BF16)],
        compiler_params=params(),
        cost_estimate=cost(0.01),
        name="back",
    )(index, out_grad, weight, *deps)


def merge_kernel(count, *refs):
    keeps, recvs = refs[:count], refs[count : 2 * count]
    keep_out, send_out = refs[2 * count :]
    half = keep_out.shape[0]
    place = 0
    for keep_ref, recv_ref in zip(keeps, recvs):
        cols = slice(place, place + keep_ref.shape[1])
        place += keep_ref.shape[1]
        total = (keep_ref[...].astype(F32) + recv_ref[...].astype(F32)).astype(BF16)
        keep_out[:, cols] = total[:half]
        send_out[:, cols] = total[half:]


def merge(keeps, recvs, deps):
    count = len(keeps)
    half = jax.ShapeDtypeStruct((keeps[0].shape[0] // 2, sum(x.shape[1] for x in keeps)), BF16)
    return pl.pallas_call(
        with_deps(functools.partial(merge_kernel, count), 2 * count, deps),
        out_shape=[half, half],
        in_specs=vmem(2 * count) + anywhere(deps),
        out_specs=vmem(2),
        compiler_params=params(),
        cost_estimate=cost(0.01),
        name="merge",
    )(*keeps, *recvs, *deps)


def load_block(block_ref, halves, order, b, nb, part, me):
    per = len(order) // 2
    for p, j in enumerate(order):
        source = halves[p // per]
        start = ((p % per) * nb + b) * part
        block_ref[row_block(me ^ j, part), :] = source[start : start + part, :]


def forward_kernel(count, *refs):
    weight_ref, out_ref = refs[count:]
    tile = jnp.concatenate([ref[...] for ref in refs[:count]], axis=0)
    out_ref[...] = jnp.dot(tile, weight_ref[...], preferred_element_type=F32)


def forward(pieces, weight, deps):
    count = len(pieces)
    return pl.pallas_call(
        with_deps(functools.partial(forward_kernel, count), count + 1, deps),
        out_shape=jax.ShapeDtypeStruct((pieces[0].shape[0] * count, weight.shape[1]), F32),
        in_specs=vmem(count + 1) + anywhere(deps),
        out_specs=pl.BlockSpec(memory_space=pltpu.VMEM),
        compiler_params=params(),
        cost_estimate=cost(0.01),
        name="forward",
    )(*pieces, weight, *deps)


def project_kernel(nt, nb, index_ref, sum_ref, near_delta, far_delta, near_ref, far_ref, out_ref, acc_ref, block_ref, slab_ref):
    me = lax.axis_index("tensor")
    order = gather_order(nt)
    rows = sum_ref.shape[0] // nt
    heads = out_ref.shape[1] // HEAD_DIM
    part = HEAD_DIM // nt
    half = nt // 2
    acc_ref[...] = sum_ref[...]
    head_of = scalars(index_ref, 1, nb)
    for b in range(nb):
        head = head_of[b]

        @pl.when(head // heads == me)
        def _():
            load_block(block_ref, (near_delta, far_delta), order, b, nb, part, me)
            for p in range(nt):
                source = near_ref if p < half else far_ref
                start = ((p % half) * nb + b) * rows
                slab_ref[p * rows : (p + 1) * rows, :] = source[start : start + rows, :]
            cols = lane_block(head - me * heads)
            acc_ref[:, cols] += jnp.dot(slab_ref[...], block_ref[...], preferred_element_type=F32)

    for p, j in enumerate(order):
        out_ref[row_block(me ^ j, rows), :] = acc_ref[p * rows : (p + 1) * rows, :].astype(BF16)


def project(index, total, near_delta, far_delta, near, far, nt, deps):
    nb = index.shape[1]
    rows, cols = total.shape
    return pl.pallas_call(
        with_deps(functools.partial(project_kernel, nt, nb), 6, deps),
        out_shape=jax.ShapeDtypeStruct((rows, cols), BF16),
        in_specs=vmem(6) + anywhere(deps),
        out_specs=pl.BlockSpec(memory_space=pltpu.VMEM),
        scratch_shapes=[
            pltpu.VMEM((rows, cols), F32),
            pltpu.VMEM((HEAD_DIM, HEAD_DIM), BF16),
            pltpu.VMEM((rows, LANES), BF16),
        ],
        compiler_params=params(),
        cost_estimate=cost(0.01),
        name="project",
    )(index, total, near_delta, far_delta, near, far, *deps)


def correct_kernel(nt, nb, chunks, index_ref, near_ref, far_ref, *refs):
    keeps, recvs = refs[:chunks], refs[chunks : 2 * chunks - 1]
    out_ref, block_ref = refs[2 * chunks - 1 :]
    me = lax.axis_index("tensor")
    order = gather_order(nt)
    part = HEAD_DIM // nt
    width = out_ref.shape[1] // chunks
    for c in range(chunks):
        cols = slice(c * width, (c + 1) * width)
        own = keeps[c][:, :width].astype(F32)
        out_ref[:, cols] = own + recvs[c][:, :width].astype(F32) if c < chunks - 1 else own
    row_of = scalars(index_ref, 0, nb)
    for b in range(nb):
        load_block(block_ref.at[b], (near_ref, far_ref), order, b, nb, part, me)
        ride = slice(width + b * LANES, width + (b + 1) * LANES)
        pick = (keeps[0][:, ride].astype(F32) + recvs[0][:, ride].astype(F32)).astype(BF16)
        out_ref[:, lane_block(row_of[b])] += lax.dot_general(
            pick, block_ref[b], (((1,), (1,)), ((), ())), preferred_element_type=F32
        )


def correct(index, near, far, keeps, recvs, depth, nt, deps):
    nb = index.shape[1]
    chunks = len(keeps)
    rows = keeps[0].shape[0]
    return pl.pallas_call(
        with_deps(functools.partial(correct_kernel, nt, nb, chunks), 2 + 2 * chunks, deps),
        out_shape=jax.ShapeDtypeStruct((rows, depth), F32),
        in_specs=vmem(2 + 2 * chunks) + anywhere(deps),
        out_specs=pl.BlockSpec(memory_space=pltpu.VMEM),
        scratch_shapes=[pltpu.VMEM((nb, HEAD_DIM, HEAD_DIM), BF16)],
        compiler_params=params(),
        cost_estimate=cost(0.01),
        name="correct",
    )(index, near, far, *keeps, *recvs, *deps)


def final_kernel(sum_ref, recv_ref, out_ref):
    width = recv_ref.shape[1]
    done = out_ref.shape[1] - width
    out_ref[:, :done] = sum_ref[:, :done].astype(BF16)
    out_ref[:, done:] = (sum_ref[:, done:] + recv_ref[...].astype(F32)).astype(BF16)


def final(total, recv, deps):
    return pl.pallas_call(
        with_deps(final_kernel, 2, deps),
        out_shape=jax.ShapeDtypeStruct(total.shape, BF16),
        in_specs=vmem(2) + anywhere(deps),
        out_specs=pl.BlockSpec(memory_space=pltpu.VMEM),
        compiler_params=params(),
        cost_estimate=cost(0.01),
        name="final",
    )(total, recv, *deps)


def on_device(tokens, base_weight, out_grad, block_index, block_owner, delta, moment1, moment2):
    nt = lax.axis_size("tensor")
    nd = lax.axis_size("dp")
    cap = delta.shape[0]
    part = HEAD_DIM // nt
    outer = bits_of(nt)[1:]
    dp_bits = bits_of(nd)[:1] + bits_of(nd)[:0:-1]
    index = block_index.T
    owner = block_owner.reshape(1, -1)

    per = BACK_PIECES // BACK_CHUNKS
    steps = len(dp_bits)

    size = index.shape[1] * tokens.shape[0]
    own = slabs(index, tokens, delta, [begin()])
    for bit in outer:
        near_slabs, lines = spread(own, xor_permute(own, "tensor", bit), size, [])
        if bit != outer[-1]:
            own = jnp.concatenate([near_slabs, lines], 0)
            size *= 2
    far_slabs = xor_permute(near_slabs, "tensor", 1)
    crossed = [tokens]
    for bit in outer:
        crossed = crossed + [xor_permute(x, "tensor", bit) for x in crossed]
    far_tokens = xor_permute(tokens, "tensor", 1)

    pieces, sums = {}, {}
    grads = {}
    got = {}
    order = []

    def tie(array):
        order.append(array)

    def deps():
        return order[-1:]

    def task_back(i):
        keep, send = back(index, out_grad, base_weight, i, i == per - 1, nt, deps())
        tie(send)
        pieces[i] = (keep, xor_permute(send, "tensor", 1))

    def task_sum(c):
        group = range(c * per, (c + 1) * per)
        for i in group:
            need("back", i)
        keep, send = merge([pieces[i][0] for i in group], [pieces[i][1] for i in group], deps())
        tie(send)
        for bit in outer[:-1]:
            keep, send = merge([keep], [xor_permute(send, "tensor", bit)], [])
        sums[c] = (keep, xor_permute(send, "tensor", outer[-1]))

    def task_grad(i):
        if i == 0:
            keep, send = block_grads(index, owner, near_slabs, far_slabs, out_grad, nt, dp_bits, cap, deps())
            grads[i] = (keep, xor_permute(send, "tensor", 1))
        else:
            need("grad", i - 1)
            keep, *way = grads[i - 1]
            bit = (dp_bits + outer)[i - 1]
            axis = "dp" if i <= steps else "tensor"
            if i == 1:
                keep, send = first_step(keep, *way, lines, deps())
                grads[i] = (keep, send, xor_permute(send, axis, bit))
            elif i <= steps:
                keep, send = step(keep, *way, deps())
                grads[i] = (keep, send, xor_permute(send, axis, bit))
            elif i == steps + 1:
                keep, send, near = compact(owner, keep, *way, dp_bits, cap, part, nt // 2, deps())
                got["delta"] = (near, xor_permute(near, "tensor", 1))
                grads[i] = (keep, xor_permute(send, axis, bit))
            else:
                keep, send = halve(keep, *way, deps())
                grads[i] = (keep, xor_permute(send, axis, bit))
        tie(send)

    def task_relay(i):
        parts = relay(crossed[1:], deps())
        tie(parts[0])
        got["tokens"] = crossed[:1] + parts + [far_tokens] + [xor_permute(x, "tensor", 1) for x in parts]

    def task_forward(i):
        need("relay", 0)
        got["total"] = forward(got["tokens"], base_weight, deps())
        tie(got["total"])

    def task_project(i):
        need("grad", steps + 1)
        need("forward", 0)
        got["projected"] = project(index, got["total"], *got["delta"], near_slabs, far_slabs, nt, deps())

    def task_correct(i):
        need("grad", steps + 1)
        for c in range(BACK_CHUNKS):
            need("sum", c)
        keeps, recvs = zip(*[sums[c] for c in range(BACK_CHUNKS)])
        got["corrected"] = correct(index, *got["delta"], keeps, recvs[:-1], tokens.shape[1], nt, deps())
        tie(got["corrected"])

    def task_adam(i):
        need("grad", steps + len(outer))
        got["adam"] = adam(*grads[steps + len(outer)], delta, moment1, moment2, deps())

    def task_final(i):
        need("correct", 0)
        got["input_grad"] = final(got["corrected"], sums[BACK_CHUNKS - 1][1], deps())

    tasks = {
        "back": task_back, "sum": task_sum, "grad": task_grad, "relay": task_relay, "project": task_project,
        "forward": task_forward, "correct": task_correct, "adam": task_adam, "final": task_final,
    }
    run = set()

    def need(name, i):
        if (name, i) not in run:
            run.add((name, i))
            tasks[name](i)

    for name, i in ORDER:
        need(name, i)
    new_delta, first_new, second_new = got["adam"]
    return (got["projected"], got["input_grad"], new_delta, first_new, second_new)


def solution(mesh):
    placed = (
        P(("dp", "tensor"), None),
        P(None, "tensor"),
        P("dp", "tensor"),
        P(),
        P(),
        P("dp", "tensor"),
        P("dp", "tensor"),
        P("dp", "tensor"),
    )
    return jax.shard_map(
        on_device,
        mesh=mesh,
        in_specs=placed,
        out_specs=(
            P("dp", "tensor"),
            P(("dp", "tensor"), None),
            P("dp", "tensor"),
            P("dp", "tensor"),
            P("dp", "tensor"),
        ),
        check_vma=False,
    )
```

```python
import functools
import math

import jax
import jax.numpy as jnp
from jax import lax
from jax.experimental import pallas as pl
from jax.experimental.pallas import tpu as pltpu
from jax.sharding import PartitionSpec as P

HEAD_DIM = 128
LANES = 128
CORRECT_ONE = 1.0 - 0.9**10
CORRECT_TWO = 1.0 - 0.999**10
BF16 = jnp.bfloat16
F32 = jnp.float32
VMEM_LIMIT = 24 * 1024 * 1024
BACK_PIECES = 4
BACK_CHUNKS = 2
ORDER = (
    ("delta", 0), ("back", 0), ("delta", 1), ("back", 1), ("delta", 2), ("sum", 0), ("relay", 0), ("back", 2), ("grad", 0), ("back", 3), ("grad", 1), ("sum", 1), ("grad", 2), ("forward", 0), ("delta", 3), ("grad", 3), ("correct", 0), ("project", 0), ("grad", 4), ("final", 0), ("adam", 0),
)


def params():
    return pltpu.CompilerParams(vmem_limit_bytes=VMEM_LIMIT)


def cost(us):
    return pl.CostEstimate(flops=int(us * 1e9), bytes_accessed=int(us * 1e6), transcendentals=0)


def vmem(n=1):
    return [pl.BlockSpec(memory_space=pltpu.VMEM)] * n


def anywhere(deps):
    return [pl.BlockSpec(memory_space=pl.ANY)] * len(deps)


def with_deps(kernel, inputs, deps):
    def run(*refs):
        kernel(*refs[:inputs], *refs[inputs + len(deps) :])

    return run


def bits_of(count):
    return [1 << i for i in range(count.bit_length() - 1)]


def halving_order(count):
    order = [0]
    for bit in reversed(bits_of(count)):
        order = order + [j + bit for j in order]
    width = count.bit_length() - 1
    rev = lambda j: int(format(j, "0%db" % width)[::-1], 2) if width else 0
    return sorted(range(count), key=rev)


def gather_order(nt):
    order = [0]
    for bit in bits_of(nt)[1:] + [1]:
        order = order + [j ^ bit for j in order]
    return order


def xor_permute(x, axis, bit):
    count = lax.axis_size(axis)
    return lax.ppermute(x, axis, [(i, i ^ bit) for i in range(count)])


def slot_ranks(owners):
    ranks = []
    for b, owner in enumerate(owners):
        rank = jnp.int32(0)
        for before in owners[:b]:
            rank = rank + (before == owner).astype(jnp.int32)
        ranks.append(rank)
    return ranks


def scalars(ref, row, nb):
    table = ref[...]
    return [table[row, b] for b in range(nb)]


def place_of(offset, bits):
    place = jnp.int32(0)
    for i, bit in enumerate(bits):
        place = place + jnp.where((offset & bit) != 0, 1 << i, 0)
    return place


def lane_block(index):
    return pl.ds(pl.multiple_of(index * LANES, LANES), LANES)


def row_block(index, rows):
    return pl.ds(pl.multiple_of(index * rows, rows), rows)


def relay_kernel(count, *refs):
    for i in range(count):
        refs[count + i][...] = refs[i][...]


def relay(parts, deps):
    count = len(parts)
    return list(
        pl.pallas_call(
            with_deps(functools.partial(relay_kernel, count), count, deps),
            out_shape=[jax.ShapeDtypeStruct(x.shape, x.dtype) for x in parts],
            in_specs=vmem(count) + anywhere(deps),
            out_specs=vmem(count),
            compiler_params=params(),
            cost_estimate=cost(10),
            name="relay",
        )(*parts, *deps)
    )


def begin_kernel(out_ref):
    out_ref[...] = jnp.zeros_like(out_ref)


def begin():
    return pl.pallas_call(
        begin_kernel,
        out_shape=jax.ShapeDtypeStruct((8, LANES), F32),
        out_specs=pl.BlockSpec(memory_space=pltpu.VMEM),
        compiler_params=params(),
        cost_estimate=cost(30),
        name="begin",
    )()


def line_kernel(delta_ref, out_ref):
    cap = delta_ref.shape[0]
    part = delta_ref.shape[1] // LANES
    delta = delta_ref[...].astype(F32)
    for k in range(cap):
        lines = [delta[k : k + 1, i * LANES : (i + 1) * LANES] for i in range(part)]
        out_ref[k * part : (k + 1) * part, :] = jnp.concatenate(lines, 0).astype(BF16)


def lines_of(delta, deps):
    return pl.pallas_call(
        with_deps(line_kernel, 1, deps),
        out_shape=jax.ShapeDtypeStruct((delta.size // LANES, LANES), BF16),
        in_specs=vmem() + anywhere(deps),
        out_specs=pl.BlockSpec(memory_space=pltpu.VMEM),
        compiler_params=params(),
        cost_estimate=cost(30),
        name="lines",
    )(delta, *deps)


def double_kernel(own_ref, recv_ref, out_ref):
    rows = own_ref.shape[0]
    out_ref[:rows, :] = own_ref[...]
    out_ref[rows:, :] = recv_ref[...]


def double(own, recv, deps):
    rows = own.shape[0]
    return pl.pallas_call(
        with_deps(double_kernel, 2, deps),
        out_shape=jax.ShapeDtypeStruct((2 * rows, LANES), BF16),
        in_specs=vmem(2) + anywhere(deps),
        out_specs=pl.BlockSpec(memory_space=pltpu.VMEM),
        compiler_params=params(),
        cost_estimate=cost(10),
        name="double",
    )(own, recv, *deps)


def compact_kernel(bits, nb, cap, part, owner_ref, own_ref, recv_ref, out_ref, all_ref):
    dp = lax.axis_index("dp")
    rows = own_ref.shape[0]
    all_ref[:rows, :] = own_ref[...]
    all_ref[rows:, :] = recv_ref[...]
    owners = scalars(owner_ref, 0, nb)
    ranks = slot_ranks(owners)
    for b in range(nb):
        start = (place_of(owners[b] ^ dp, bits) * cap + ranks[b]) * part
        out_ref[b * part : (b + 1) * part, :] = all_ref[pl.ds(pl.multiple_of(start, part), part), :]


def compact(owner, own, recv, bits, cap, part, deps):
    nb = owner.shape[1]
    return pl.pallas_call(
        with_deps(functools.partial(compact_kernel, bits, nb, cap, part), 3, deps),
        out_shape=jax.ShapeDtypeStruct((nb * part, LANES), BF16),
        in_specs=vmem(3) + anywhere(deps),
        out_specs=pl.BlockSpec(memory_space=pltpu.VMEM),
        scratch_shapes=[pltpu.VMEM((2 * own.shape[0], LANES), BF16)],
        compiler_params=params(),
        cost_estimate=cost(10),
        name="compact_step",
    )(owner, own, recv, *deps)


def unride_kernel(part, width, own_ref, recv_ref, out_ref):
    rows = own_ref.shape[0]
    out_ref[:rows, :] = own_ref[...]
    for b in range(rows // part):
        cols = slice(width + b * LANES, width + (b + 1) * LANES)
        out_ref[rows + b * part : rows + (b + 1) * part, :] = recv_ref[:part, cols]


def unride(own, recv, part, deps):
    rows = own.shape[0]
    width = recv.shape[1] - rows // part * LANES
    return pl.pallas_call(
        with_deps(functools.partial(unride_kernel, part, width), 2, deps),
        out_shape=jax.ShapeDtypeStruct((2 * rows, LANES), BF16),
        in_specs=vmem(2) + anywhere(deps),
        out_specs=pl.BlockSpec(memory_space=pltpu.VMEM),
        compiler_params=params(),
        cost_estimate=cost(10),
        name="unride",
    )(own, recv, *deps)


def grad_kernel(nt, bits, nb, cap, scale, index_ref, owner_ref, grad_ref, *refs):
    token_refs = refs[:nt]
    keep_ref, send_ref, slab_ref, block_ref = refs[nt:]
    me = lax.axis_index("tensor")
    dp = lax.axis_index("dp")
    part = HEAD_DIM // nt
    rows = grad_ref.shape[0] // nt
    heads = grad_ref.shape[1] // HEAD_DIM
    half = nt // 2
    keep_ref[...] = jnp.zeros_like(keep_ref)
    send_ref[...] = jnp.zeros_like(send_ref)
    owners = scalars(owner_ref, 0, nb)
    ranks = slot_ranks(owners)
    row_of = scalars(index_ref, 0, nb)
    head_of = scalars(index_ref, 1, nb)
    for b in range(nb):
        head = head_of[b]

        @pl.when(head // heads == me)
        def _():
            for ref, j in zip(token_refs, gather_order(nt)):
                slab_ref[row_block(me ^ j, rows), :] = ref[:, lane_block(row_of[b])]
            block_ref[...] = (
                lax.dot_general(
                    slab_ref[...],
                    grad_ref[:, lane_block(head - me * heads)],
                    (((0,), (0,)), ((), ())),
                    preferred_element_type=F32,
                )
                * scale
            ).astype(BF16)
            place = place_of(owners[b] ^ dp, bits[::-1])
            for p, j in enumerate(halving_order(nt)):
                target = keep_ref if p < half else send_ref
                start = ((place * half + p % half) * cap + ranks[b]) * part
                target[pl.ds(pl.multiple_of(start, part), part), :] = block_ref[row_block(me ^ j, part), :]


def block_grads(index, owner, out_grad, pieces, nt, bits, cap, deps):
    nb = index.shape[1]
    rows = out_grad.shape[0]
    nd = 1 << len(bits)
    scale = 1.0 / math.sqrt(rows * nd)
    size = nd * (nt // 2) * cap * (HEAD_DIM // nt)
    half = jax.ShapeDtypeStruct((size, LANES), BF16)
    return pl.pallas_call(
        with_deps(functools.partial(grad_kernel, nt, bits, nb, cap, scale), 3 + nt, deps),
        out_shape=[half, half],
        in_specs=vmem(3 + nt) + anywhere(deps),
        out_specs=vmem(2),
        scratch_shapes=[pltpu.VMEM((rows, LANES), BF16), pltpu.VMEM((HEAD_DIM, HEAD_DIM), BF16)],
        compiler_params=params(),
        cost_estimate=cost(10),
        name="block_grads",
    )(index, owner, out_grad, *pieces, *deps)


def halve_kernel(keep_ref, recv_ref, keep_out, send_out):
    half = keep_out.shape[0]
    total = (keep_ref[...].astype(F32) + recv_ref[...].astype(F32)).astype(BF16)
    keep_out[...] = total[:half]
    send_out[...] = total[half:]


def halve(keep, recv, deps):
    rows = keep.shape[0]
    half = jax.ShapeDtypeStruct((rows // 2, LANES), BF16)
    return pl.pallas_call(
        with_deps(halve_kernel, 2, deps),
        out_shape=[half, half],
        in_specs=vmem(2) + anywhere(deps),
        out_specs=vmem(2),
        compiler_params=params(),
        cost_estimate=cost(10),
        name="halve",
    )(keep, recv, *deps)


def adam_kernel(
    cap, keep_ref, recv_ref, delta_ref, one_ref, two_ref, delta_out, one_out, two_out, grad_ref
):
    part = keep_ref.shape[0] // cap
    total = keep_ref[...].astype(F32) + recv_ref[...].astype(F32)
    for k in range(cap):
        for i in range(part):
            grad_ref[k : k + 1, i * LANES : (i + 1) * LANES] = total[k * part + i : k * part + i + 1, :]
    grad = grad_ref[...]
    first = 0.9 * one_ref[...] + 0.1 * grad
    second = 0.999 * two_ref[...] + 0.001 * grad * grad
    one_out[...] = first
    two_out[...] = second
    update = 0.02 * (first / CORRECT_ONE) / (jnp.sqrt(second / CORRECT_TWO) + 1e-08)
    delta_out[...] = (delta_ref[...].astype(F32) - update).astype(BF16)


def adam(keep, recv, delta, moment1, moment2, deps):
    return pl.pallas_call(
        with_deps(functools.partial(adam_kernel, delta.shape[0]), 5, deps),
        out_shape=[
            jax.ShapeDtypeStruct(delta.shape, BF16),
            jax.ShapeDtypeStruct(delta.shape, F32),
            jax.ShapeDtypeStruct(delta.shape, F32),
        ],
        in_specs=vmem(5) + anywhere(deps),
        out_specs=vmem(3),
        scratch_shapes=[pltpu.VMEM(delta.shape, F32)],
        compiler_params=params(),
        cost_estimate=cost(10),
        name="adam",
    )(keep, recv, delta, moment1, moment2, *deps)


def back_kernel(nt, nb, start, width, index_ref, grad_ref, weight_ref, keep_ref, send_ref, perm_ref):
    me = lax.axis_index("tensor")
    rows = grad_ref.shape[0] // nt
    heads = grad_ref.shape[1] // HEAD_DIM
    half = nt // 2 * rows
    for p, j in enumerate(halving_order(nt)):
        perm_ref[p * rows : (p + 1) * rows, :] = grad_ref[row_block(me ^ j, rows), :]
    out = lax.dot_general(
        weight_ref[start : start + width, :], perm_ref[...], (((1,), (1,)), ((), ())), preferred_element_type=F32
    )
    out = out.astype(BF16).T
    keep_ref[:, :width] = out[:half]
    send_ref[:, :width] = out[half:]
    if keep_ref.shape[1] > width:
        head_of = scalars(index_ref, 1, nb)
        for b in range(nb):
            head = head_of[b]
            mine = head // heads == me
            part = perm_ref[:, lane_block(jnp.where(mine, head - me * heads, 0))]
            part = jnp.where(mine, part, jnp.zeros_like(part))
            cols = slice(width + b * LANES, width + (b + 1) * LANES)
            keep_ref[:, cols] = part[:half]
            send_ref[:, cols] = part[half:]


def back(index, out_grad, weight, piece, riders, nt, deps):
    nb = index.shape[1]
    rows = out_grad.shape[0]
    depth = weight.shape[0]
    width = depth // BACK_PIECES
    half = jax.ShapeDtypeStruct((rows // 2, width + (nb * LANES if riders else 0)), BF16)
    return pl.pallas_call(
        with_deps(functools.partial(back_kernel, nt, nb, piece * width, width), 3, deps),
        out_shape=[half, half],
        in_specs=vmem(3) + anywhere(deps),
        out_specs=vmem(2),
        scratch_shapes=[pltpu.VMEM(out_grad.shape, BF16)],
        compiler_params=params(),
        cost_estimate=cost(10),
        name="back",
    )(index, out_grad, weight, *deps)


def merge_kernel(count, part, *refs):
    keeps, recvs = refs[:count], refs[count : 2 * count]
    keep_out, send_out = refs[-2:]
    half = keep_out.shape[0]
    place = 0
    for keep_ref, recv_ref in zip(keeps, recvs):
        cols = slice(place, place + keep_ref.shape[1])
        place += keep_ref.shape[1]
        total = (keep_ref[...].astype(F32) + recv_ref[...].astype(F32)).astype(BF16)
        keep_out[:, cols] = total[:half]
        send_out[:, cols] = total[half:]
    for rider_ref in refs[2 * count : -2]:
        for b in range(rider_ref.shape[0] // part):
            cols = slice(place + b * LANES, place + (b + 1) * LANES)
            send_out[:part, cols] = rider_ref[b * part : (b + 1) * part, :]
            if part < half:
                send_out[part:, cols] = jnp.zeros((half - part, LANES), BF16)


def merge(keeps, recvs, riders, part, deps):
    count = len(keeps)
    rows = keeps[0].shape[0] // 2
    width = sum(x.shape[1] for x in keeps)
    extra = sum(x.shape[0] for x in riders) // part * LANES
    return pl.pallas_call(
        with_deps(functools.partial(merge_kernel, count, part), 2 * count + len(riders), deps),
        out_shape=[jax.ShapeDtypeStruct((rows, width), BF16), jax.ShapeDtypeStruct((rows, width + extra), BF16)],
        in_specs=vmem(2 * count + len(riders)) + anywhere(deps),
        out_specs=vmem(2),
        compiler_params=params(),
        cost_estimate=cost(10),
        name="merge",
    )(*keeps, *recvs, *riders, *deps)


def load_block(block_ref, halves, order, b, nb, part, me):
    per = len(order) // 2
    for p, j in enumerate(order):
        source = halves[p // per]
        start = ((p % per) * nb + b) * part
        block_ref[row_block(me ^ j, part), :] = source[start : start + part, :]


def forward_kernel(count, *refs):
    weight_ref, out_ref = refs[count:]
    tile = jnp.concatenate([ref[...] for ref in refs[:count]], axis=0)
    out_ref[...] = jnp.dot(tile, weight_ref[...], preferred_element_type=F32)


def forward(pieces, weight, deps):
    count = len(pieces)
    return pl.pallas_call(
        with_deps(functools.partial(forward_kernel, count), count + 1, deps),
        out_shape=jax.ShapeDtypeStruct((pieces[0].shape[0] * count, weight.shape[1]), F32),
        in_specs=vmem(count + 1) + anywhere(deps),
        out_specs=pl.BlockSpec(memory_space=pltpu.VMEM),
        compiler_params=params(),
        cost_estimate=cost(10),
        name="forward",
    )(*pieces, weight, *deps)


def project_kernel(nt, nb, index_ref, sum_ref, near_delta, far_delta, *refs):
    token_refs = refs[:nt]
    out_ref, acc_ref, block_ref = refs[nt:]
    me = lax.axis_index("tensor")
    order = gather_order(nt)
    rows = sum_ref.shape[0] // nt
    heads = out_ref.shape[1] // HEAD_DIM
    part = HEAD_DIM // nt
    acc_ref[...] = sum_ref[...]
    row_of = scalars(index_ref, 0, nb)
    head_of = scalars(index_ref, 1, nb)
    for b in range(nb):
        head = head_of[b]

        @pl.when(head // heads == me)
        def _():
            load_block(block_ref, (near_delta, far_delta), order, b, nb, part, me)
            slab = jnp.concatenate([ref[:, lane_block(row_of[b])] for ref in token_refs], axis=0)
            cols = lane_block(head - me * heads)
            acc_ref[:, cols] += jnp.dot(slab, block_ref[...], preferred_element_type=F32)

    for p, j in enumerate(order):
        out_ref[row_block(me ^ j, rows), :] = acc_ref[p * rows : (p + 1) * rows, :].astype(BF16)


def project(index, total, near_delta, far_delta, pieces, nt, deps):
    nb = index.shape[1]
    rows, cols = total.shape
    return pl.pallas_call(
        with_deps(functools.partial(project_kernel, nt, nb), 4 + nt, deps),
        out_shape=jax.ShapeDtypeStruct((rows, cols), BF16),
        in_specs=vmem(4 + nt) + anywhere(deps),
        out_specs=pl.BlockSpec(memory_space=pltpu.VMEM),
        scratch_shapes=[pltpu.VMEM((rows, cols), F32), pltpu.VMEM((HEAD_DIM, HEAD_DIM), BF16)],
        compiler_params=params(),
        cost_estimate=cost(10),
        name="project",
    )(index, total, near_delta, far_delta, *pieces, *deps)


def correct_kernel(nt, nb, chunks, index_ref, near_ref, far_ref, *refs):
    keeps, recvs = refs[:chunks], refs[chunks : 2 * chunks - 1]
    out_ref, block_ref = refs[2 * chunks - 1 :]
    me = lax.axis_index("tensor")
    order = gather_order(nt)
    part = HEAD_DIM // nt
    width = out_ref.shape[1] // chunks
    for c in range(chunks):
        cols = slice(c * width, (c + 1) * width)
        own = keeps[c][:, :width].astype(F32)
        out_ref[:, cols] = own + recvs[c][:, :width].astype(F32) if c < chunks - 1 else own
    row_of = scalars(index_ref, 0, nb)
    for b in range(nb):
        load_block(block_ref.at[b], (near_ref, far_ref), order, b, nb, part, me)
        ride = slice(width + b * LANES, width + (b + 1) * LANES)
        pick = (keeps[0][:, ride].astype(F32) + recvs[0][:, ride].astype(F32)).astype(BF16)
        out_ref[:, lane_block(row_of[b])] += lax.dot_general(
            pick, block_ref[b], (((1,), (1,)), ((), ())), preferred_element_type=F32
        )


def correct(index, near, far, keeps, recvs, depth, nt, deps):
    nb = index.shape[1]
    chunks = len(keeps)
    rows = keeps[0].shape[0]
    return pl.pallas_call(
        with_deps(functools.partial(correct_kernel, nt, nb, chunks), 2 + 2 * chunks, deps),
        out_shape=jax.ShapeDtypeStruct((rows, depth), F32),
        in_specs=vmem(2 + 2 * chunks) + anywhere(deps),
        out_specs=pl.BlockSpec(memory_space=pltpu.VMEM),
        scratch_shapes=[pltpu.VMEM((nb, HEAD_DIM, HEAD_DIM), BF16)],
        compiler_params=params(),
        cost_estimate=cost(10),
        name="correct",
    )(index, near, far, *keeps, *recvs, *deps)


def final_kernel(sum_ref, recv_ref, out_ref):
    width = out_ref.shape[1] // BACK_CHUNKS
    done = out_ref.shape[1] - width
    out_ref[:, :done] = sum_ref[:, :done].astype(BF16)
    out_ref[:, done:] = (sum_ref[:, done:] + recv_ref[:, :width].astype(F32)).astype(BF16)


def final(total, recv, deps):
    return pl.pallas_call(
        with_deps(final_kernel, 2, deps),
        out_shape=jax.ShapeDtypeStruct(total.shape, BF16),
        in_specs=vmem(2) + anywhere(deps),
        out_specs=pl.BlockSpec(memory_space=pltpu.VMEM),
        compiler_params=params(),
        cost_estimate=cost(10),
        name="final",
    )(total, recv, *deps)


def on_device(tokens, base_weight, out_grad, block_index, block_owner, delta, moment1, moment2):
    nt = lax.axis_size("tensor")
    nd = lax.axis_size("dp")
    cap = delta.shape[0]
    part = HEAD_DIM // nt
    outer = bits_of(nt)[1:]
    grad_bits = bits_of(nd)
    delta_bits = grad_bits[:1] + grad_bits[:0:-1]
    grad_ways = [("tensor", 1)] + [("dp", bit) for bit in grad_bits] + [("tensor", bit) for bit in outer]
    index = block_index.T
    owner = block_owner.reshape(1, -1)
    per = BACK_PIECES // BACK_CHUNKS
    last_chunk = BACK_CHUNKS - 1

    crossed = [tokens]
    for bit in outer:
        crossed = crossed + [xor_permute(x, "tensor", bit) for x in crossed]
    far_tokens = xor_permute(tokens, "tensor", 1)

    lines = lines_of(delta, [begin()])
    order = [lines]
    pieces, sums, grads, got = {}, {}, {}, {}
    deltas = {0: (lines, xor_permute(lines, "dp", delta_bits[0]))}

    def tie(array):
        order.append(array)

    def deps():
        return order[-1:]

    def task_delta(i):
        if i > 0:
            need("delta", i - 1)
        if i < len(delta_bits) - 1:
            lines = double(*deltas[i], deps())
            tie(lines)
            deltas[i + 1] = (lines, xor_permute(lines, "dp", delta_bits[i + 1]))
        elif i == len(delta_bits) - 1:
            blocks = compact(owner, *deltas[i], delta_bits, cap, part, deps())
            tie(blocks)
            for bit in outer[:-1]:
                blocks = double(blocks, xor_permute(blocks, "tensor", bit), [])
            got["blocks"] = blocks
        else:
            need("sum", 0)
            near = unride(got["blocks"], sums[0][1], part, deps())
            tie(near)
            got["delta"] = (near, xor_permute(near, "tensor", 1))

    def task_back(i):
        keep, send = back(index, out_grad, base_weight, i, i == per - 1, nt, deps())
        tie(send)
        pieces[i] = (keep, xor_permute(send, "tensor", 1))

    def task_sum(c):
        group = range(c * per, (c + 1) * per)
        for i in group:
            need("back", i)
        riders = []
        if c == 0:
            need("delta", len(delta_bits) - 1)
            riders = [got["blocks"]]
        keeps, recvs = [pieces[i][0] for i in group], [pieces[i][1] for i in group]
        for i, bit in enumerate(outer):
            early = deps() if i == 0 else []
            keep, send = merge(keeps, recvs, riders if bit == outer[-1] else [], part, early)
            keeps, recvs = [keep], [xor_permute(send, "tensor", bit)]
        tie(keep)
        sums[c] = (keep, recvs[0])

    def task_grad(i):
        if i == 0:
            need("relay", 0)
            keep, send = block_grads(index, owner, out_grad, got["tokens"], nt, grad_bits, cap, deps())
        else:
            need("grad", i - 1)
            keep, send = halve(*grads[i - 1], deps())
        tie(send)
        grads[i] = (keep, xor_permute(send, *grad_ways[i]))

    def task_relay(i):
        parts = relay(crossed[1:], deps())
        tie(parts[0])
        got["tokens"] = crossed[:1] + parts + [far_tokens] + [xor_permute(x, "tensor", 1) for x in parts]

    def task_forward(i):
        need("relay", 0)
        got["total"] = forward(got["tokens"], base_weight, deps())
        tie(got["total"])

    def task_project(i):
        need("delta", len(delta_bits))
        need("forward", 0)
        got["projected"] = project(index, got["total"], *got["delta"], got["tokens"], nt, deps())

    def task_correct(i):
        need("delta", len(delta_bits))
        for c in range(BACK_CHUNKS):
            need("sum", c)
        keeps, recvs = zip(*[sums[c] for c in range(BACK_CHUNKS)])
        got["corrected"] = correct(index, *got["delta"], keeps, recvs[:-1], tokens.shape[1], nt, deps())
        tie(got["corrected"])

    def task_adam(i):
        need("grad", len(grad_ways) - 1)
        got["adam"] = adam(*grads[len(grad_ways) - 1], delta, moment1, moment2, deps())

    def task_final(i):
        need("correct", 0)
        got["input_grad"] = final(got["corrected"], sums[last_chunk][1], deps())

    tasks = {
        "delta": task_delta, "back": task_back, "sum": task_sum, "grad": task_grad, "relay": task_relay,
        "forward": task_forward, "project": task_project, "correct": task_correct, "adam": task_adam, "final": task_final,
    }
    run = set()

    def need(name, i):
        if (name, i) not in run:
            run.add((name, i))
            tasks[name](i)

    for name, i in ORDER:
        need(name, i)
    new_delta, first_new, second_new = got["adam"]
    return (got["projected"], got["input_grad"], new_delta, first_new, second_new)


def solution(mesh):
    placed = (
        P(("dp", "tensor"), None),
        P(None, "tensor"),
        P("dp", "tensor"),
        P(),
        P(),
        P("dp", "tensor"),
        P("dp", "tensor"),
        P("dp", "tensor"),
    )
    return jax.shard_map(
        on_device,
        mesh=mesh,
        in_specs=placed,
        out_specs=(
            P("dp", "tensor"),
            P(("dp", "tensor"), None),
            P("dp", "tensor"),
            P("dp", "tensor"),
            P("dp", "tensor"),
        ),
        check_vma=False,
    )
```

```python
import functools
import math

import jax
import jax.numpy as jnp
from jax import lax
from jax.experimental import pallas as pl
from jax.experimental.pallas import tpu as pltpu
from jax.sharding import PartitionSpec as P

HEAD_DIM = 128
LANES = 128
CORRECT_ONE = 1.0 - 0.9**10
CORRECT_TWO = 1.0 - 0.999**10
BF16 = jnp.bfloat16
F32 = jnp.float32
VMEM_LIMIT = 24 * 1024 * 1024
BACK_PIECES = 4
BACK_CHUNKS = 2
PAUSE = 30
FIRST = 30
ORDER = (
    ("back", 0), ("delta", 0), ("back", 1), ("back", 2), ("sum", 0), ("relay", 0), ("back", 3), ("grad", 0), ("delta", 1), ("grad", 1), ("sum", 1), ("grad", 2), ("forward", 0), ("grad", 3), ("delta", 3), ("grad", 4), ("correct", 0), ("project", 0), ("final", 0), ("adam", 0),
)


def params():
    return pltpu.CompilerParams(vmem_limit_bytes=VMEM_LIMIT)


def cost(us):
    return pl.CostEstimate(flops=int(us * 1e9), bytes_accessed=int(us * 1e6), transcendentals=0)


def vmem(n=1):
    return [pl.BlockSpec(memory_space=pltpu.VMEM)] * n


def anywhere(deps):
    return [pl.BlockSpec(memory_space=pl.ANY)] * len(deps)


def with_deps(kernel, inputs, deps):
    def run(*refs):
        kernel(*refs[:inputs], *refs[inputs + len(deps) :])

    return run


def bits_of(count):
    return [1 << i for i in range(count.bit_length() - 1)]


def halving_order(count):
    order = [0]
    for bit in reversed(bits_of(count)):
        order = order + [j + bit for j in order]
    width = count.bit_length() - 1
    rev = lambda j: int(format(j, "0%db" % width)[::-1], 2) if width else 0
    return sorted(range(count), key=rev)


def gather_order(nt):
    order = [0]
    for bit in bits_of(nt)[1:] + [1]:
        order = order + [j ^ bit for j in order]
    return order


def xor_permute(x, axis, bit):
    count = lax.axis_size(axis)
    return lax.ppermute(x, axis, [(i, i ^ bit) for i in range(count)])


def slot_ranks(owners):
    ranks = []
    for b, owner in enumerate(owners):
        rank = jnp.int32(0)
        for before in owners[:b]:
            rank = rank + (before == owner).astype(jnp.int32)
        ranks.append(rank)
    return ranks


def scalars(ref, row, nb):
    table = ref[...]
    return [table[row, b] for b in range(nb)]


def place_of(offset, bits):
    place = jnp.int32(0)
    for i, bit in enumerate(bits):
        place = place + jnp.where((offset & bit) != 0, 1 << i, 0)
    return place


def lane_block(index):
    return pl.ds(pl.multiple_of(index * LANES, LANES), LANES)


def row_block(index, rows):
    return pl.ds(pl.multiple_of(index * rows, rows), rows)


def relay_kernel(count, *refs):
    for i in range(count):
        refs[count + i][...] = refs[i][...]


def relay(parts, deps, us=10):
    count = len(parts)
    return list(
        pl.pallas_call(
            with_deps(functools.partial(relay_kernel, count), count, deps),
            out_shape=[jax.ShapeDtypeStruct(x.shape, x.dtype) for x in parts],
            in_specs=vmem(count) + anywhere(deps),
            out_specs=vmem(count),
            compiler_params=params(),
            cost_estimate=cost(us),
            name="relay",
        )(*parts, *deps)
    )


def pause_kernel(out_ref):
    out_ref[...] = jnp.zeros_like(out_ref)


def pause(deps, us):
    return pl.pallas_call(
        with_deps(pause_kernel, 0, deps),
        out_shape=jax.ShapeDtypeStruct((8, LANES), F32),
        in_specs=anywhere(deps),
        out_specs=pl.BlockSpec(memory_space=pltpu.VMEM),
        compiler_params=params(),
        cost_estimate=cost(us),
        name="pause",
    )(*deps)


def line_kernel(delta_ref, out_ref):
    cap = delta_ref.shape[0]
    part = delta_ref.shape[1] // LANES
    delta = delta_ref[...].astype(F32)
    for k in range(cap):
        lines = [delta[k : k + 1, i * LANES : (i + 1) * LANES] for i in range(part)]
        out_ref[k * part : (k + 1) * part, :] = jnp.concatenate(lines, 0).astype(BF16)


def lines_of(delta, deps):
    return pl.pallas_call(
        with_deps(line_kernel, 1, deps),
        out_shape=jax.ShapeDtypeStruct((delta.size // LANES, LANES), BF16),
        in_specs=vmem() + anywhere(deps),
        out_specs=pl.BlockSpec(memory_space=pltpu.VMEM),
        compiler_params=params(),
        cost_estimate=cost(30),
        name="lines",
    )(delta, *deps)


def double_kernel(own_ref, recv_ref, out_ref):
    rows = own_ref.shape[0]
    out_ref[:rows, :] = own_ref[...]
    out_ref[rows:, :] = recv_ref[...]


def double(own, recv, deps):
    rows = own.shape[0]
    return pl.pallas_call(
        with_deps(double_kernel, 2, deps),
        out_shape=jax.ShapeDtypeStruct((2 * rows, LANES), BF16),
        in_specs=vmem(2) + anywhere(deps),
        out_specs=pl.BlockSpec(memory_space=pltpu.VMEM),
        compiler_params=params(),
        cost_estimate=cost(10),
        name="double",
    )(own, recv, *deps)


def compact_kernel(bits, nb, cap, part, owner_ref, own_ref, recv_ref, out_ref, all_ref):
    dp = lax.axis_index("dp")
    rows = own_ref.shape[0]
    all_ref[:rows, :] = own_ref[...]
    all_ref[rows:, :] = recv_ref[...]
    owners = scalars(owner_ref, 0, nb)
    ranks = slot_ranks(owners)
    for b in range(nb):
        start = (place_of(owners[b] ^ dp, bits) * cap + ranks[b]) * part
        out_ref[b * part : (b + 1) * part, :] = all_ref[pl.ds(pl.multiple_of(start, part), part), :]


def compact(owner, own, recv, bits, cap, part, deps):
    nb = owner.shape[1]
    return pl.pallas_call(
        with_deps(functools.partial(compact_kernel, bits, nb, cap, part), 3, deps),
        out_shape=jax.ShapeDtypeStruct((nb * part, LANES), BF16),
        in_specs=vmem(3) + anywhere(deps),
        out_specs=pl.BlockSpec(memory_space=pltpu.VMEM),
        scratch_shapes=[pltpu.VMEM((2 * own.shape[0], LANES), BF16)],
        compiler_params=params(),
        cost_estimate=cost(10),
        name="compact_step",
    )(owner, own, recv, *deps)


def unride_kernel(part, width, own_ref, recv_ref, out_ref):
    rows = own_ref.shape[0]
    out_ref[:rows, :] = own_ref[...]
    for b in range(rows // part):
        cols = slice(width + b * LANES, width + (b + 1) * LANES)
        out_ref[rows + b * part : rows + (b + 1) * part, :] = recv_ref[:part, cols]


def unride(own, recv, part, deps):
    rows = own.shape[0]
    width = recv.shape[1] - rows // part * LANES
    return pl.pallas_call(
        with_deps(functools.partial(unride_kernel, part, width), 2, deps),
        out_shape=jax.ShapeDtypeStruct((2 * rows, LANES), BF16),
        in_specs=vmem(2) + anywhere(deps),
        out_specs=pl.BlockSpec(memory_space=pltpu.VMEM),
        compiler_params=params(),
        cost_estimate=cost(10),
        name="unride",
    )(own, recv, *deps)


def grad_kernel(nt, bits, nb, cap, scale, index_ref, owner_ref, grad_ref, *refs):
    token_refs = refs[:nt]
    keep_ref, send_ref, slab_ref, block_ref = refs[nt:]
    me = lax.axis_index("tensor")
    dp = lax.axis_index("dp")
    part = HEAD_DIM // nt
    rows = grad_ref.shape[0] // nt
    heads = grad_ref.shape[1] // HEAD_DIM
    half = nt // 2
    keep_ref[...] = jnp.zeros_like(keep_ref)
    send_ref[...] = jnp.zeros_like(send_ref)
    owners = scalars(owner_ref, 0, nb)
    ranks = slot_ranks(owners)
    row_of = scalars(index_ref, 0, nb)
    head_of = scalars(index_ref, 1, nb)
    for b in range(nb):
        head = head_of[b]

        @pl.when(head // heads == me)
        def _():
            for ref, j in zip(token_refs, gather_order(nt)):
                slab_ref[row_block(me ^ j, rows), :] = ref[:, lane_block(row_of[b])]
            block_ref[...] = (
                lax.dot_general(
                    slab_ref[...],
                    grad_ref[:, lane_block(head - me * heads)],
                    (((0,), (0,)), ((), ())),
                    preferred_element_type=F32,
                )
                * scale
            ).astype(BF16)
            place = place_of(owners[b] ^ dp, bits[::-1])
            for p, j in enumerate(halving_order(nt)):
                target = keep_ref if p < half else send_ref
                start = ((place * half + p % half) * cap + ranks[b]) * part
                target[pl.ds(pl.multiple_of(start, part), part), :] = block_ref[row_block(me ^ j, part), :]


def block_grads(index, owner, out_grad, pieces, nt, bits, cap, deps):
    nb = index.shape[1]
    rows = out_grad.shape[0]
    nd = 1 << len(bits)
    scale = 1.0 / math.sqrt(rows * nd)
    size = nd * (nt // 2) * cap * (HEAD_DIM // nt)
    half = jax.ShapeDtypeStruct((size, LANES), BF16)
    return pl.pallas_call(
        with_deps(functools.partial(grad_kernel, nt, bits, nb, cap, scale), 3 + nt, deps),
        out_shape=[half, half],
        in_specs=vmem(3 + nt) + anywhere(deps),
        out_specs=vmem(2),
        scratch_shapes=[pltpu.VMEM((rows, LANES), BF16), pltpu.VMEM((HEAD_DIM, HEAD_DIM), BF16)],
        compiler_params=params(),
        cost_estimate=cost(10),
        name="block_grads",
    )(index, owner, out_grad, *pieces, *deps)


def halve_kernel(keep_ref, recv_ref, keep_out, send_out):
    half = keep_out.shape[0]
    total = (keep_ref[...].astype(F32) + recv_ref[...].astype(F32)).astype(BF16)
    keep_out[...] = total[:half]
    send_out[...] = total[half:]


def halve(keep, recv, deps):
    rows = keep.shape[0]
    half = jax.ShapeDtypeStruct((rows // 2, LANES), BF16)
    return pl.pallas_call(
        with_deps(halve_kernel, 2, deps),
        out_shape=[half, half],
        in_specs=vmem(2) + anywhere(deps),
        out_specs=vmem(2),
        compiler_params=params(),
        cost_estimate=cost(10),
        name="halve",
    )(keep, recv, *deps)


def adam_kernel(
    cap, keep_ref, recv_ref, delta_ref, one_ref, two_ref, delta_out, one_out, two_out, grad_ref
):
    part = keep_ref.shape[0] // cap
    total = keep_ref[...].astype(F32) + recv_ref[...].astype(F32)
    for k in range(cap):
        for i in range(part):
            grad_ref[k : k + 1, i * LANES : (i + 1) * LANES] = total[k * part + i : k * part + i + 1, :]
    grad = grad_ref[...]
    first = 0.9 * one_ref[...] + 0.1 * grad
    second = 0.999 * two_ref[...] + 0.001 * grad * grad
    one_out[...] = first
    two_out[...] = second
    update = 0.02 * (first / CORRECT_ONE) / (jnp.sqrt(second / CORRECT_TWO) + 1e-08)
    delta_out[...] = (delta_ref[...].astype(F32) - update).astype(BF16)


def adam(keep, recv, delta, moment1, moment2, deps):
    return pl.pallas_call(
        with_deps(functools.partial(adam_kernel, delta.shape[0]), 5, deps),
        out_shape=[
            jax.ShapeDtypeStruct(delta.shape, BF16),
            jax.ShapeDtypeStruct(delta.shape, F32),
            jax.ShapeDtypeStruct(delta.shape, F32),
        ],
        in_specs=vmem(5) + anywhere(deps),
        out_specs=vmem(3),
        scratch_shapes=[pltpu.VMEM(delta.shape, F32)],
        compiler_params=params(),
        cost_estimate=cost(10),
        name="adam",
    )(keep, recv, delta, moment1, moment2, *deps)


def back_kernel(nt, nb, start, width, index_ref, grad_ref, weight_ref, keep_ref, send_ref, perm_ref):
    me = lax.axis_index("tensor")
    rows = grad_ref.shape[0] // nt
    heads = grad_ref.shape[1] // HEAD_DIM
    half = nt // 2 * rows
    for p, j in enumerate(halving_order(nt)):
        perm_ref[p * rows : (p + 1) * rows, :] = grad_ref[row_block(me ^ j, rows), :]
    out = lax.dot_general(
        weight_ref[start : start + width, :], perm_ref[...], (((1,), (1,)), ((), ())), preferred_element_type=F32
    )
    out = out.astype(BF16).T
    keep_ref[:, :width] = out[:half]
    send_ref[:, :width] = out[half:]
    if keep_ref.shape[1] > width:
        head_of = scalars(index_ref, 1, nb)
        for b in range(nb):
            head = head_of[b]
            mine = head // heads == me
            part = perm_ref[:, lane_block(jnp.where(mine, head - me * heads, 0))]
            part = jnp.where(mine, part, jnp.zeros_like(part))
            cols = slice(width + b * LANES, width + (b + 1) * LANES)
            keep_ref[:, cols] = part[:half]
            send_ref[:, cols] = part[half:]


def back(index, out_grad, weight, piece, riders, nt, deps):
    nb = index.shape[1]
    rows = out_grad.shape[0]
    depth = weight.shape[0]
    width = depth // BACK_PIECES
    half = jax.ShapeDtypeStruct((rows // 2, width + (nb * LANES if riders else 0)), BF16)
    return pl.pallas_call(
        with_deps(functools.partial(back_kernel, nt, nb, piece * width, width), 3, deps),
        out_shape=[half, half],
        in_specs=vmem(3) + anywhere(deps),
        out_specs=vmem(2),
        scratch_shapes=[pltpu.VMEM(out_grad.shape, BF16)],
        compiler_params=params(),
        cost_estimate=cost(10),
        name="back",
    )(index, out_grad, weight, *deps)


def merge_kernel(count, part, *refs):
    keeps, recvs = refs[:count], refs[count : 2 * count]
    keep_out, send_out = refs[-2:]
    half = keep_out.shape[0]
    place = 0
    for keep_ref, recv_ref in zip(keeps, recvs):
        cols = slice(place, place + keep_ref.shape[1])
        place += keep_ref.shape[1]
        total = (keep_ref[...].astype(F32) + recv_ref[...].astype(F32)).astype(BF16)
        keep_out[:, cols] = total[:half]
        send_out[:, cols] = total[half:]
    for rider_ref in refs[2 * count : -2]:
        for b in range(rider_ref.shape[0] // part):
            cols = slice(place + b * LANES, place + (b + 1) * LANES)
            send_out[:part, cols] = rider_ref[b * part : (b + 1) * part, :]
            if part < half:
                send_out[part:, cols] = jnp.zeros((half - part, LANES), BF16)


def merge(keeps, recvs, riders, part, deps):
    count = len(keeps)
    rows = keeps[0].shape[0] // 2
    width = sum(x.shape[1] for x in keeps)
    extra = sum(x.shape[0] for x in riders) // part * LANES
    return pl.pallas_call(
        with_deps(functools.partial(merge_kernel, count, part), 2 * count + len(riders), deps),
        out_shape=[jax.ShapeDtypeStruct((rows, width), BF16), jax.ShapeDtypeStruct((rows, width + extra), BF16)],
        in_specs=vmem(2 * count + len(riders)) + anywhere(deps),
        out_specs=vmem(2),
        compiler_params=params(),
        cost_estimate=cost(10),
        name="merge",
    )(*keeps, *recvs, *riders, *deps)


def load_block(block_ref, halves, order, b, nb, part, me):
    per = len(order) // 2
    for p, j in enumerate(order):
        source = halves[p // per]
        start = ((p % per) * nb + b) * part
        block_ref[row_block(me ^ j, part), :] = source[start : start + part, :]


def forward_kernel(count, *refs):
    weight_ref, out_ref = refs[count:]
    tile = jnp.concatenate([ref[...] for ref in refs[:count]], axis=0)
    out_ref[...] = jnp.dot(tile, weight_ref[...], preferred_element_type=F32)


def forward(pieces, weight, deps):
    count = len(pieces)
    return pl.pallas_call(
        with_deps(functools.partial(forward_kernel, count), count + 1, deps),
        out_shape=jax.ShapeDtypeStruct((pieces[0].shape[0] * count, weight.shape[1]), F32),
        in_specs=vmem(count + 1) + anywhere(deps),
        out_specs=pl.BlockSpec(memory_space=pltpu.VMEM),
        compiler_params=params(),
        cost_estimate=cost(10),
        name="forward",
    )(*pieces, weight, *deps)


def project_kernel(nt, nb, index_ref, sum_ref, near_delta, far_delta, *refs):
    token_refs = refs[:nt]
    out_ref, acc_ref, block_ref = refs[nt:]
    me = lax.axis_index("tensor")
    order = gather_order(nt)
    rows = sum_ref.shape[0] // nt
    heads = out_ref.shape[1] // HEAD_DIM
    part = HEAD_DIM // nt
    acc_ref[...] = sum_ref[...]
    row_of = scalars(index_ref, 0, nb)
    head_of = scalars(index_ref, 1, nb)
    for b in range(nb):
        head = head_of[b]

        @pl.when(head // heads == me)
        def _():
            load_block(block_ref, (near_delta, far_delta), order, b, nb, part, me)
            slab = jnp.concatenate([ref[:, lane_block(row_of[b])] for ref in token_refs], axis=0)
            cols = lane_block(head - me * heads)
            acc_ref[:, cols] += jnp.dot(slab, block_ref[...], preferred_element_type=F32)

    for p, j in enumerate(order):
        out_ref[row_block(me ^ j, rows), :] = acc_ref[p * rows : (p + 1) * rows, :].astype(BF16)


def project(index, total, near_delta, far_delta, pieces, nt, deps):
    nb = index.shape[1]
    rows, cols = total.shape
    return pl.pallas_call(
        with_deps(functools.partial(project_kernel, nt, nb), 4 + nt, deps),
        out_shape=jax.ShapeDtypeStruct((rows, cols), BF16),
        in_specs=vmem(4 + nt) + anywhere(deps),
        out_specs=pl.BlockSpec(memory_space=pltpu.VMEM),
        scratch_shapes=[pltpu.VMEM((rows, cols), F32), pltpu.VMEM((HEAD_DIM, HEAD_DIM), BF16)],
        compiler_params=params(),
        cost_estimate=cost(10),
        name="project",
    )(index, total, near_delta, far_delta, *pieces, *deps)


def correct_kernel(nt, nb, chunks, index_ref, near_ref, far_ref, *refs):
    keeps, recvs = refs[:chunks], refs[chunks : 2 * chunks - 1]
    out_ref, block_ref = refs[2 * chunks - 1 :]
    me = lax.axis_index("tensor")
    order = gather_order(nt)
    part = HEAD_DIM // nt
    width = out_ref.shape[1] // chunks
    for c in range(chunks):
        cols = slice(c * width, (c + 1) * width)
        own = keeps[c][:, :width].astype(F32)
        out_ref[:, cols] = own + recvs[c][:, :width].astype(F32) if c < chunks - 1 else own
    row_of = scalars(index_ref, 0, nb)
    for b in range(nb):
        load_block(block_ref.at[b], (near_ref, far_ref), order, b, nb, part, me)
        ride = slice(width + b * LANES, width + (b + 1) * LANES)
        pick = (keeps[0][:, ride].astype(F32) + recvs[0][:, ride].astype(F32)).astype(BF16)
        out_ref[:, lane_block(row_of[b])] += lax.dot_general(
            pick, block_ref[b], (((1,), (1,)), ((), ())), preferred_element_type=F32
        )


def correct(index, near, far, keeps, recvs, depth, nt, deps):
    nb = index.shape[1]
    chunks = len(keeps)
    rows = keeps[0].shape[0]
    return pl.pallas_call(
        with_deps(functools.partial(correct_kernel, nt, nb, chunks), 2 + 2 * chunks, deps),
        out_shape=jax.ShapeDtypeStruct((rows, depth), F32),
        in_specs=vmem(2 + 2 * chunks) + anywhere(deps),
        out_specs=pl.BlockSpec(memory_space=pltpu.VMEM),
        scratch_shapes=[pltpu.VMEM((nb, HEAD_DIM, HEAD_DIM), BF16)],
        compiler_params=params(),
        cost_estimate=cost(10),
        name="correct",
    )(index, near, far, *keeps, *recvs, *deps)


def final_kernel(sum_ref, recv_ref, out_ref):
    width = out_ref.shape[1] // BACK_CHUNKS
    done = out_ref.shape[1] - width
    out_ref[:, :done] = sum_ref[:, :done].astype(BF16)
    out_ref[:, done:] = (sum_ref[:, done:] + recv_ref[:, :width].astype(F32)).astype(BF16)


def final(total, recv, deps):
    return pl.pallas_call(
        with_deps(final_kernel, 2, deps),
        out_shape=jax.ShapeDtypeStruct(total.shape, BF16),
        in_specs=vmem(2) + anywhere(deps),
        out_specs=pl.BlockSpec(memory_space=pltpu.VMEM),
        compiler_params=params(),
        cost_estimate=cost(10),
        name="final",
    )(total, recv, *deps)


def on_device(tokens, base_weight, out_grad, block_index, block_owner, delta, moment1, moment2):
    nt = lax.axis_size("tensor")
    nd = lax.axis_size("dp")
    cap = delta.shape[0]
    part = HEAD_DIM // nt
    outer = bits_of(nt)[1:]
    grad_bits = bits_of(nd)
    delta_bits = grad_bits[:1] + grad_bits[:0:-1]
    grad_ways = [("tensor", 1)] + [("dp", bit) for bit in grad_bits] + [("tensor", bit) for bit in outer]
    index = block_index.T
    owner = block_owner.reshape(1, -1)
    per = BACK_PIECES // BACK_CHUNKS
    last_chunk = BACK_CHUNKS - 1

    (own,) = relay([tokens], [pause([], PAUSE)], FIRST)
    crossed = [own]
    for bit in outer:
        crossed = crossed + [xor_permute(x, "tensor", bit) for x in crossed]
    far_tokens = xor_permute(own, "tensor", 1)

    lines = lines_of(delta, [own])
    order = [pause([lines], 3)]
    pieces, sums, grads, got = {}, {}, {}, {}
    deltas = {0: (lines, xor_permute(lines, "dp", delta_bits[0]))}

    def tie(array):
        order.append(array)

    def deps():
        return order[-1:]

    def task_delta(i):
        if i > 0:
            need("delta", i - 1)
        if i < len(delta_bits) - 1:
            lines = double(*deltas[i], deps())
            tie(lines)
            deltas[i + 1] = (lines, xor_permute(lines, "dp", delta_bits[i + 1]))
        elif i == len(delta_bits) - 1:
            blocks = compact(owner, *deltas[i], delta_bits, cap, part, deps())
            tie(blocks)
            for bit in outer[:-1]:
                blocks = double(blocks, xor_permute(blocks, "tensor", bit), [])
            got["blocks"] = blocks
        else:
            need("sum", last_chunk)
            near = unride(got["blocks"], sums[last_chunk][1], part, deps())
            tie(near)
            got["delta"] = (near, xor_permute(near, "tensor", 1))

    def task_back(i):
        keep, send = back(index, out_grad, base_weight, i, i == per - 1, nt, deps())
        tie(send)
        pieces[i] = (keep, xor_permute(send, "tensor", 1))

    def task_sum(c):
        group = range(c * per, (c + 1) * per)
        for i in group:
            need("back", i)
        riders = []
        if c == last_chunk:
            need("delta", len(delta_bits) - 1)
            riders = [got["blocks"]]
        keeps, recvs = [pieces[i][0] for i in group], [pieces[i][1] for i in group]
        for i, bit in enumerate(outer):
            early = deps() if i == 0 else []
            keep, send = merge(keeps, recvs, riders if bit == outer[-1] else [], part, early)
            keeps, recvs = [keep], [xor_permute(send, "tensor", bit)]
        tie(keep)
        sums[c] = (keep, recvs[0])

    def task_grad(i):
        if i == 0:
            need("relay", 0)
            keep, send = block_grads(index, owner, out_grad, got["tokens"], nt, grad_bits, cap, deps())
        else:
            need("grad", i - 1)
            keep, send = halve(*grads[i - 1], deps())
        tie(send)
        grads[i] = (keep, xor_permute(send, *grad_ways[i]))

    def task_relay(i):
        parts = relay(crossed[1:], deps())
        tie(parts[0])
        got["tokens"] = crossed[:1] + parts + [far_tokens] + [xor_permute(x, "tensor", 1) for x in parts]

    def task_forward(i):
        need("relay", 0)
        got["total"] = forward(got["tokens"], base_weight, deps())
        tie(got["total"])

    def task_project(i):
        need("delta", len(delta_bits))
        need("forward", 0)
        got["projected"] = project(index, got["total"], *got["delta"], got["tokens"], nt, deps())

    def task_correct(i):
        need("delta", len(delta_bits))
        for c in range(BACK_CHUNKS):
            need("sum", c)
        keeps, recvs = zip(*[sums[c] for c in range(BACK_CHUNKS)])
        got["corrected"] = correct(index, *got["delta"], keeps, recvs[:-1], tokens.shape[1], nt, deps())
        tie(got["corrected"])

    def task_adam(i):
        need("grad", len(grad_ways) - 1)
        got["adam"] = adam(*grads[len(grad_ways) - 1], delta, moment1, moment2, deps())

    def task_final(i):
        need("correct", 0)
        got["input_grad"] = final(got["corrected"], sums[last_chunk][1], deps())

    tasks = {
        "delta": task_delta, "back": task_back, "sum": task_sum, "grad": task_grad, "relay": task_relay,
        "forward": task_forward, "project": task_project, "correct": task_correct, "adam": task_adam, "final": task_final,
    }
    run = set()

    def need(name, i):
        if (name, i) not in run:
            run.add((name, i))
            tasks[name](i)

    for name, i in ORDER:
        need(name, i)
    new_delta, first_new, second_new = got["adam"]
    return (got["projected"], got["input_grad"], new_delta, first_new, second_new)


def solution(mesh):
    placed = (
        P(("dp", "tensor"), None),
        P(None, "tensor"),
        P("dp", "tensor"),
        P(),
        P(),
        P("dp", "tensor"),
        P("dp", "tensor"),
        P("dp", "tensor"),
    )
    return jax.shard_map(
        on_device,
        mesh=mesh,
        in_specs=placed,
        out_specs=(
            P("dp", "tensor"),
            P(("dp", "tensor"), None),
            P("dp", "tensor"),
            P("dp", "tensor"),
            P("dp", "tensor"),
        ),
        check_vma=False,
    )
```

```python
import functools
import math

import jax
import jax.numpy as jnp
from jax import lax
from jax.experimental import pallas as pl
from jax.experimental.pallas import tpu as pltpu
from jax.sharding import PartitionSpec as P

HEAD_DIM = 128
LANES = 128
CORRECT_ONE = 1.0 - 0.9**10
CORRECT_TWO = 1.0 - 0.999**10
BF16 = jnp.bfloat16
F32 = jnp.float32
VMEM_LIMIT = 24 * 1024 * 1024
BACK_PIECES = 4
BACK_CHUNKS = 2
PAUSE = 30
FIRST = 30
ORDER = (
    ("back", 0), ("delta", 0), ("back", 1), ("back", 2), ("sum", 0), ("relay", 0), ("back", 3), ("grad", 0), ("delta", 1), ("grad", 1), ("sum", 1), ("grad", 2), ("forward", 0), ("grad", 3), ("delta", 3), ("grad", 4), ("correct", 0), ("project", 0), ("final", 0), ("adam", 0),
)


def params():
    return pltpu.CompilerParams(vmem_limit_bytes=VMEM_LIMIT)


def cost(us):
    return pl.CostEstimate(flops=int(us * 1e9), bytes_accessed=int(us * 1e6), transcendentals=0)


def vmem(n=1):
    return [pl.BlockSpec(memory_space=pltpu.VMEM)] * n


def anywhere(deps):
    return [pl.BlockSpec(memory_space=pl.ANY)] * len(deps)


def with_deps(kernel, inputs, deps):
    def run(*refs):
        kernel(*refs[:inputs], *refs[inputs + len(deps) :])

    return run


def bits_of(count):
    return [1 << i for i in range(count.bit_length() - 1)]


def halving_order(count):
    order = [0]
    for bit in reversed(bits_of(count)):
        order = order + [j + bit for j in order]
    width = count.bit_length() - 1
    rev = lambda j: int(format(j, "0%db" % width)[::-1], 2) if width else 0
    return sorted(range(count), key=rev)


def gather_order(nt):
    order = [0]
    for bit in bits_of(nt)[1:] + [1]:
        order = order + [j ^ bit for j in order]
    return order


def xor_permute(x, axis, bit):
    count = lax.axis_size(axis)
    return lax.ppermute(x, axis, [(i, i ^ bit) for i in range(count)])


def slot_ranks(owners):
    ranks = []
    for b, owner in enumerate(owners):
        rank = jnp.int32(0)
        for before in owners[:b]:
            rank = rank + (before == owner).astype(jnp.int32)
        ranks.append(rank)
    return ranks


def scalars(ref, row, nb):
    table = ref[...]
    return [table[row, b] for b in range(nb)]


def place_of(offset, bits):
    place = jnp.int32(0)
    for i, bit in enumerate(bits):
        place = place + jnp.where((offset & bit) != 0, 1 << i, 0)
    return place


def lane_block(index):
    return pl.ds(pl.multiple_of(index * LANES, LANES), LANES)


def row_block(index, rows):
    return pl.ds(pl.multiple_of(index * rows, rows), rows)


def relay_kernel(count, *refs):
    for i in range(count):
        refs[count + i][...] = refs[i][...]


def relay(parts, deps, us=10):
    count = len(parts)
    return list(
        pl.pallas_call(
            with_deps(functools.partial(relay_kernel, count), count, deps),
            out_shape=[jax.ShapeDtypeStruct(x.shape, x.dtype) for x in parts],
            in_specs=vmem(count) + anywhere(deps),
            out_specs=vmem(count),
            compiler_params=params(),
            cost_estimate=cost(us),
            name="relay",
        )(*parts, *deps)
    )


def pause_kernel(out_ref):
    out_ref[...] = jnp.zeros_like(out_ref)


def pause(deps, us):
    return pl.pallas_call(
        with_deps(pause_kernel, 0, deps),
        out_shape=jax.ShapeDtypeStruct((8, LANES), F32),
        in_specs=anywhere(deps),
        out_specs=pl.BlockSpec(memory_space=pltpu.VMEM),
        compiler_params=params(),
        cost_estimate=cost(us),
        name="pause",
    )(*deps)


def line_kernel(delta_ref, out_ref):
    cap = delta_ref.shape[0]
    part = delta_ref.shape[1] // LANES
    delta = delta_ref[...].astype(F32)
    for k in range(cap):
        lines = [delta[k : k + 1, i * LANES : (i + 1) * LANES] for i in range(part)]
        out_ref[k * part : (k + 1) * part, :] = jnp.concatenate(lines, 0).astype(BF16)


def lines_of(delta, deps):
    return pl.pallas_call(
        with_deps(line_kernel, 1, deps),
        out_shape=jax.ShapeDtypeStruct((delta.size // LANES, LANES), BF16),
        in_specs=vmem() + anywhere(deps),
        out_specs=pl.BlockSpec(memory_space=pltpu.VMEM),
        compiler_params=params(),
        cost_estimate=cost(30),
        name="lines",
    )(delta, *deps)


def double_kernel(own_ref, recv_ref, out_ref):
    rows = own_ref.shape[0]
    out_ref[:rows, :] = own_ref[...]
    out_ref[rows:, :] = recv_ref[...]


def double(own, recv, deps):
    rows = own.shape[0]
    return pl.pallas_call(
        with_deps(double_kernel, 2, deps),
        out_shape=jax.ShapeDtypeStruct((2 * rows, LANES), BF16),
        in_specs=vmem(2) + anywhere(deps),
        out_specs=pl.BlockSpec(memory_space=pltpu.VMEM),
        compiler_params=params(),
        cost_estimate=cost(10),
        name="double",
    )(own, recv, *deps)


def compact_kernel(bits, nb, cap, part, owner_ref, own_ref, recv_ref, out_ref, all_ref):
    dp = lax.axis_index("dp")
    rows = own_ref.shape[0]
    all_ref[:rows, :] = own_ref[...]
    all_ref[rows:, :] = recv_ref[...]
    owners = scalars(owner_ref, 0, nb)
    ranks = slot_ranks(owners)
    for b in range(nb):
        start = (place_of(owners[b] ^ dp, bits) * cap + ranks[b]) * part
        out_ref[b * part : (b + 1) * part, :] = all_ref[pl.ds(pl.multiple_of(start, part), part), :]


def compact(owner, own, recv, bits, cap, part, deps):
    nb = owner.shape[1]
    return pl.pallas_call(
        with_deps(functools.partial(compact_kernel, bits, nb, cap, part), 3, deps),
        out_shape=jax.ShapeDtypeStruct((nb * part, LANES), BF16),
        in_specs=vmem(3) + anywhere(deps),
        out_specs=pl.BlockSpec(memory_space=pltpu.VMEM),
        scratch_shapes=[pltpu.VMEM((2 * own.shape[0], LANES), BF16)],
        compiler_params=params(),
        cost_estimate=cost(10),
        name="compact_step",
    )(owner, own, recv, *deps)


def unride_kernel(part, width, own_ref, recv_ref, out_ref):
    rows = own_ref.shape[0]
    out_ref[:rows, :] = own_ref[...]
    for b in range(rows // part):
        cols = slice(width + b * LANES, width + (b + 1) * LANES)
        out_ref[rows + b * part : rows + (b + 1) * part, :] = recv_ref[:part, cols]


def unride(own, recv, part, deps):
    rows = own.shape[0]
    width = recv.shape[1] - rows // part * LANES
    return pl.pallas_call(
        with_deps(functools.partial(unride_kernel, part, width), 2, deps),
        out_shape=jax.ShapeDtypeStruct((2 * rows, LANES), BF16),
        in_specs=vmem(2) + anywhere(deps),
        out_specs=pl.BlockSpec(memory_space=pltpu.VMEM),
        compiler_params=params(),
        cost_estimate=cost(10),
        name="unride",
    )(own, recv, *deps)


def grad_kernel(nt, bits, nb, cap, scale, index_ref, owner_ref, grad_ref, *refs):
    token_refs = refs[:nt]
    keep_ref, send_ref, slab_ref, block_ref = refs[nt:]
    me = lax.axis_index("tensor")
    dp = lax.axis_index("dp")
    part = HEAD_DIM // nt
    rows = grad_ref.shape[0] // nt
    heads = grad_ref.shape[1] // HEAD_DIM
    half = nt // 2
    keep_ref[...] = jnp.zeros_like(keep_ref)
    send_ref[...] = jnp.zeros_like(send_ref)
    owners = scalars(owner_ref, 0, nb)
    ranks = slot_ranks(owners)
    row_of = scalars(index_ref, 0, nb)
    head_of = scalars(index_ref, 1, nb)
    for b in range(nb):
        head = head_of[b]

        @pl.when(head // heads == me)
        def _():
            for ref, j in zip(token_refs, gather_order(nt)):
                slab_ref[row_block(me ^ j, rows), :] = ref[:, lane_block(row_of[b])]
            block_ref[...] = (
                lax.dot_general(
                    slab_ref[...],
                    grad_ref[:, lane_block(head - me * heads)],
                    (((0,), (0,)), ((), ())),
                    preferred_element_type=F32,
                )
                * scale
            ).astype(BF16)
            place = place_of(owners[b] ^ dp, bits[::-1])
            for p, j in enumerate(halving_order(nt)):
                target = keep_ref if p < half else send_ref
                start = ((place * half + p % half) * cap + ranks[b]) * part
                target[pl.ds(pl.multiple_of(start, part), part), :] = block_ref[row_block(me ^ j, part), :]


def block_grads(index, owner, out_grad, pieces, nt, bits, cap, deps):
    nb = index.shape[1]
    rows = out_grad.shape[0]
    nd = 1 << len(bits)
    scale = 1.0 / math.sqrt(rows * nd)
    size = nd * (nt // 2) * cap * (HEAD_DIM // nt)
    half = jax.ShapeDtypeStruct((size, LANES), BF16)
    return pl.pallas_call(
        with_deps(functools.partial(grad_kernel, nt, bits, nb, cap, scale), 3 + nt, deps),
        out_shape=[half, half],
        in_specs=vmem(3 + nt) + anywhere(deps),
        out_specs=vmem(2),
        scratch_shapes=[pltpu.VMEM((rows, LANES), BF16), pltpu.VMEM((HEAD_DIM, HEAD_DIM), BF16)],
        compiler_params=params(),
        cost_estimate=cost(10),
        name="block_grads",
    )(index, owner, out_grad, *pieces, *deps)


def halve_kernel(keep_ref, recv_ref, keep_out, send_out):
    half = keep_out.shape[0]
    total = (keep_ref[...].astype(F32) + recv_ref[...].astype(F32)).astype(BF16)
    keep_out[...] = total[:half]
    send_out[...] = total[half:]


def halve(keep, recv, deps):
    rows = keep.shape[0]
    half = jax.ShapeDtypeStruct((rows // 2, LANES), BF16)
    return pl.pallas_call(
        with_deps(halve_kernel, 2, deps),
        out_shape=[half, half],
        in_specs=vmem(2) + anywhere(deps),
        out_specs=vmem(2),
        compiler_params=params(),
        cost_estimate=cost(10),
        name="halve",
    )(keep, recv, *deps)


def adam_kernel(
    cap, keep_ref, recv_ref, delta_ref, one_ref, two_ref, delta_out, one_out, two_out, grad_ref
):
    part = keep_ref.shape[0] // cap
    total = keep_ref[...].astype(F32) + recv_ref[...].astype(F32)
    for k in range(cap):
        for i in range(part):
            grad_ref[k : k + 1, i * LANES : (i + 1) * LANES] = total[k * part + i : k * part + i + 1, :]
    grad = grad_ref[...]
    first = 0.9 * one_ref[...] + 0.1 * grad
    second = 0.999 * two_ref[...] + 0.001 * grad * grad
    one_out[...] = first
    two_out[...] = second
    update = 0.02 * (first / CORRECT_ONE) / (jnp.sqrt(second / CORRECT_TWO) + 1e-08)
    delta_out[...] = (delta_ref[...].astype(F32) - update).astype(BF16)


def adam(keep, recv, delta, moment1, moment2, deps):
    return pl.pallas_call(
        with_deps(functools.partial(adam_kernel, delta.shape[0]), 5, deps),
        out_shape=[
            jax.ShapeDtypeStruct(delta.shape, BF16),
            jax.ShapeDtypeStruct(delta.shape, F32),
            jax.ShapeDtypeStruct(delta.shape, F32),
        ],
        in_specs=vmem(5) + anywhere(deps),
        out_specs=vmem(3),
        scratch_shapes=[pltpu.VMEM(delta.shape, F32)],
        compiler_params=params(),
        cost_estimate=cost(10),
        name="adam",
    )(keep, recv, delta, moment1, moment2, *deps)


def back_kernel(nt, nb, start, width, index_ref, grad_ref, weight_ref, keep_ref, send_ref, perm_ref):
    me = lax.axis_index("tensor")
    rows = grad_ref.shape[0] // nt
    heads = grad_ref.shape[1] // HEAD_DIM
    half = nt // 2 * rows
    for p, j in enumerate(halving_order(nt)):
        perm_ref[p * rows : (p + 1) * rows, :] = grad_ref[row_block(me ^ j, rows), :]
    out = lax.dot_general(
        weight_ref[start : start + width, :], perm_ref[...], (((1,), (1,)), ((), ())), preferred_element_type=F32
    )
    out = out.astype(BF16).T
    keep_ref[:, :width] = out[:half]
    send_ref[:, :width] = out[half:]
    if keep_ref.shape[1] > width:
        head_of = scalars(index_ref, 1, nb)
        for b in range(nb):
            head = head_of[b]
            mine = head // heads == me
            part = perm_ref[:, lane_block(jnp.where(mine, head - me * heads, 0))]
            part = jnp.where(mine, part, jnp.zeros_like(part))
            cols = slice(width + b * LANES, width + (b + 1) * LANES)
            keep_ref[:, cols] = part[:half]
            send_ref[:, cols] = part[half:]


def back(index, out_grad, weight, piece, riders, nt, deps):
    nb = index.shape[1]
    rows = out_grad.shape[0]
    depth = weight.shape[0]
    width = depth // BACK_PIECES
    half = jax.ShapeDtypeStruct((rows // 2, width + (nb * LANES if riders else 0)), BF16)
    return pl.pallas_call(
        with_deps(functools.partial(back_kernel, nt, nb, piece * width, width), 3, deps),
        out_shape=[half, half],
        in_specs=vmem(3) + anywhere(deps),
        out_specs=vmem(2),
        scratch_shapes=[pltpu.VMEM(out_grad.shape, BF16)],
        compiler_params=params(),
        cost_estimate=cost(10),
        name="back",
    )(index, out_grad, weight, *deps)


def merge_kernel(count, part, *refs):
    keeps, recvs = refs[:count], refs[count : 2 * count]
    keep_out, send_out = refs[-2:]
    half = keep_out.shape[0]
    place = 0
    for keep_ref, recv_ref in zip(keeps, recvs):
        cols = slice(place, place + keep_ref.shape[1])
        place += keep_ref.shape[1]
        total = (keep_ref[...].astype(F32) + recv_ref[...].astype(F32)).astype(BF16)
        keep_out[:, cols] = total[:half]
        send_out[:, cols] = total[half:]
    for rider_ref in refs[2 * count : -2]:
        for b in range(rider_ref.shape[0] // part):
            cols = slice(place + b * LANES, place + (b + 1) * LANES)
            send_out[:part, cols] = rider_ref[b * part : (b + 1) * part, :]
            if part < half:
                send_out[part:, cols] = jnp.zeros((half - part, LANES), BF16)


def merge(keeps, recvs, riders, part, deps):
    count = len(keeps)
    rows = keeps[0].shape[0] // 2
    width = sum(x.shape[1] for x in keeps)
    extra = sum(x.shape[0] for x in riders) // part * LANES
    return pl.pallas_call(
        with_deps(functools.partial(merge_kernel, count, part), 2 * count + len(riders), deps),
        out_shape=[jax.ShapeDtypeStruct((rows, width), BF16), jax.ShapeDtypeStruct((rows, width + extra), BF16)],
        in_specs=vmem(2 * count + len(riders)) + anywhere(deps),
        out_specs=vmem(2),
        compiler_params=params(),
        cost_estimate=cost(10),
        name="merge",
    )(*keeps, *recvs, *riders, *deps)


def load_block(block_ref, halves, order, b, nb, part, me):
    per = len(order) // 2
    for p, j in enumerate(order):
        source = halves[p // per]
        start = ((p % per) * nb + b) * part
        block_ref[row_block(me ^ j, part), :] = source[start : start + part, :]


def forward_kernel(count, *refs):
    weight_ref, out_ref = refs[count:]
    tile = jnp.concatenate([ref[...] for ref in refs[:count]], axis=0)
    out_ref[...] = jnp.dot(tile, weight_ref[...], preferred_element_type=F32)


def forward(pieces, weight, deps):
    count = len(pieces)
    return pl.pallas_call(
        with_deps(functools.partial(forward_kernel, count), count + 1, deps),
        out_shape=jax.ShapeDtypeStruct((pieces[0].shape[0] * count, weight.shape[1]), F32),
        in_specs=vmem(count + 1) + anywhere(deps),
        out_specs=pl.BlockSpec(memory_space=pltpu.VMEM),
        compiler_params=params(),
        cost_estimate=cost(10),
        name="forward",
    )(*pieces, weight, *deps)


def project_kernel(nt, nb, index_ref, sum_ref, near_delta, far_delta, *refs):
    token_refs = refs[:nt]
    out_ref, acc_ref, block_ref = refs[nt:]
    me = lax.axis_index("tensor")
    order = gather_order(nt)
    rows = sum_ref.shape[0] // nt
    heads = out_ref.shape[1] // HEAD_DIM
    part = HEAD_DIM // nt
    acc_ref[...] = sum_ref[...]
    row_of = scalars(index_ref, 0, nb)
    head_of = scalars(index_ref, 1, nb)
    for b in range(nb):
        head = head_of[b]

        @pl.when(head // heads == me)
        def _():
            load_block(block_ref, (near_delta, far_delta), order, b, nb, part, me)
            slab = jnp.concatenate([ref[:, lane_block(row_of[b])] for ref in token_refs], axis=0)
            cols = lane_block(head - me * heads)
            acc_ref[:, cols] += jnp.dot(slab, block_ref[...], preferred_element_type=F32)

    for p, j in enumerate(order):
        out_ref[row_block(me ^ j, rows), :] = acc_ref[p * rows : (p + 1) * rows, :].astype(BF16)


def project(index, total, near_delta, far_delta, pieces, nt, deps):
    nb = index.shape[1]
    rows, cols = total.shape
    return pl.pallas_call(
        with_deps(functools.partial(project_kernel, nt, nb), 4 + nt, deps),
        out_shape=jax.ShapeDtypeStruct((rows, cols), BF16),
        in_specs=vmem(4 + nt) + anywhere(deps),
        out_specs=pl.BlockSpec(memory_space=pltpu.VMEM),
        scratch_shapes=[pltpu.VMEM((rows, cols), F32), pltpu.VMEM((HEAD_DIM, HEAD_DIM), BF16)],
        compiler_params=params(),
        cost_estimate=cost(10),
        name="project",
    )(index, total, near_delta, far_delta, *pieces, *deps)


def correct_kernel(nt, nb, chunks, index_ref, near_ref, far_ref, *refs):
    keeps, recvs = refs[:chunks], refs[chunks : 2 * chunks - 1]
    out_ref, block_ref = refs[2 * chunks - 1 :]
    me = lax.axis_index("tensor")
    order = gather_order(nt)
    part = HEAD_DIM // nt
    width = out_ref.shape[1] // chunks
    for c in range(chunks):
        cols = slice(c * width, (c + 1) * width)
        own = keeps[c][:, :width].astype(F32)
        out_ref[:, cols] = own + recvs[c][:, :width].astype(F32) if c < chunks - 1 else own
    row_of = scalars(index_ref, 0, nb)
    for b in range(nb):
        load_block(block_ref.at[b], (near_ref, far_ref), order, b, nb, part, me)
        ride = slice(width + b * LANES, width + (b + 1) * LANES)
        pick = (keeps[0][:, ride].astype(F32) + recvs[0][:, ride].astype(F32)).astype(BF16)
        out_ref[:, lane_block(row_of[b])] += lax.dot_general(
            pick, block_ref[b], (((1,), (1,)), ((), ())), preferred_element_type=F32
        )


def correct(index, near, far, keeps, recvs, depth, nt, deps):
    nb = index.shape[1]
    chunks = len(keeps)
    rows = keeps[0].shape[0]
    return pl.pallas_call(
        with_deps(functools.partial(correct_kernel, nt, nb, chunks), 2 + 2 * chunks, deps),
        out_shape=jax.ShapeDtypeStruct((rows, depth), F32),
        in_specs=vmem(2 + 2 * chunks) + anywhere(deps),
        out_specs=pl.BlockSpec(memory_space=pltpu.VMEM),
        scratch_shapes=[pltpu.VMEM((nb, HEAD_DIM, HEAD_DIM), BF16)],
        compiler_params=params(),
        cost_estimate=cost(10),
        name="correct",
    )(index, near, far, *keeps, *recvs, *deps)


def final_kernel(sum_ref, recv_ref, out_ref):
    width = out_ref.shape[1] // BACK_CHUNKS
    done = out_ref.shape[1] - width
    out_ref[:, :done] = sum_ref[:, :done].astype(BF16)
    out_ref[:, done:] = (sum_ref[:, done:] + recv_ref[:, :width].astype(F32)).astype(BF16)


def final(total, recv, deps):
    return pl.pallas_call(
        with_deps(final_kernel, 2, deps),
        out_shape=jax.ShapeDtypeStruct(total.shape, BF16),
        in_specs=vmem(2) + anywhere(deps),
        out_specs=pl.BlockSpec(memory_space=pltpu.VMEM),
        compiler_params=params(),
        cost_estimate=cost(10),
        name="final",
    )(total, recv, *deps)


def on_device(tokens, base_weight, out_grad, block_index, block_owner, delta, moment1, moment2):
    nt = lax.axis_size("tensor")
    nd = lax.axis_size("dp")
    cap = delta.shape[0]
    part = HEAD_DIM // nt
    outer = bits_of(nt)[1:]
    grad_bits = bits_of(nd)
    delta_bits = grad_bits
    grad_ways = [("tensor", 1)] + [("dp", bit) for bit in grad_bits] + [("tensor", bit) for bit in outer]
    index = block_index.T
    owner = block_owner.reshape(1, -1)
    per = BACK_PIECES // BACK_CHUNKS
    last_chunk = BACK_CHUNKS - 1

    (own,) = relay([tokens], [pause([], PAUSE)], FIRST)
    crossed = [own]
    for bit in outer:
        crossed = crossed + [xor_permute(x, "tensor", bit) for x in crossed]
    far_tokens = xor_permute(own, "tensor", 1)

    lines = lines_of(delta, [own])
    order = [pause([lines], 3)]
    pieces, sums, grads, got = {}, {}, {}, {}
    deltas = {0: (lines, xor_permute(lines, "dp", delta_bits[0]))}

    def tie(array):
        order.append(array)

    def deps():
        return order[-1:]

    def task_delta(i):
        if i > 0:
            need("delta", i - 1)
        if i < len(delta_bits) - 1:
            lines = double(*deltas[i], deps())
            tie(lines)
            deltas[i + 1] = (lines, xor_permute(lines, "dp", delta_bits[i + 1]))
        elif i == len(delta_bits) - 1:
            blocks = compact(owner, *deltas[i], delta_bits, cap, part, deps())
            tie(blocks)
            for bit in outer[:-1]:
                blocks = double(blocks, xor_permute(blocks, "tensor", bit), [])
            got["blocks"] = blocks
        else:
            need("sum", last_chunk)
            near = unride(got["blocks"], sums[last_chunk][1], part, deps())
            tie(near)
            got["delta"] = (near, xor_permute(near, "tensor", 1))

    def task_back(i):
        keep, send = back(index, out_grad, base_weight, i, i == per - 1, nt, deps())
        tie(send)
        pieces[i] = (keep, xor_permute(send, "tensor", 1))

    def task_sum(c):
        group = range(c * per, (c + 1) * per)
        for i in group:
            need("back", i)
        riders = []
        if c == last_chunk:
            need("delta", len(delta_bits) - 1)
            riders = [got["blocks"]]
        keeps, recvs = [pieces[i][0] for i in group], [pieces[i][1] for i in group]
        for i, bit in enumerate(outer):
            early = deps() if i == 0 else []
            keep, send = merge(keeps, recvs, riders if bit == outer[-1] else [], part, early)
            keeps, recvs = [keep], [xor_permute(send, "tensor", bit)]
        tie(keep)
        sums[c] = (keep, recvs[0])

    def task_grad(i):
        if i == 0:
            need("relay", 0)
            keep, send = block_grads(index, owner, out_grad, got["tokens"], nt, grad_bits, cap, deps())
        else:
            need("grad", i - 1)
            keep, send = halve(*grads[i - 1], deps())
        tie(send)
        grads[i] = (keep, xor_permute(send, *grad_ways[i]))

    def task_relay(i):
        parts = relay(crossed[1:], deps())
        tie(parts[0])
        got["tokens"] = crossed[:1] + parts + [far_tokens] + [xor_permute(x, "tensor", 1) for x in parts]

    def task_forward(i):
        need("relay", 0)
        got["total"] = forward(got["tokens"], base_weight, deps())
        tie(got["total"])

    def task_project(i):
        need("delta", len(delta_bits))
        need("forward", 0)
        got["projected"] = project(index, got["total"], *got["delta"], got["tokens"], nt, deps())

    def task_correct(i):
        need("delta", len(delta_bits))
        for c in range(BACK_CHUNKS):
            need("sum", c)
        keeps, recvs = zip(*[sums[c] for c in range(BACK_CHUNKS)])
        got["corrected"] = correct(index, *got["delta"], keeps, recvs[:-1], tokens.shape[1], nt, deps())
        tie(got["corrected"])

    def task_adam(i):
        need("grad", len(grad_ways) - 1)
        got["adam"] = adam(*grads[len(grad_ways) - 1], delta, moment1, moment2, deps())

    def task_final(i):
        need("correct", 0)
        got["input_grad"] = final(got["corrected"], sums[last_chunk][1], deps())

    tasks = {
        "delta": task_delta, "back": task_back, "sum": task_sum, "grad": task_grad, "relay": task_relay,
        "forward": task_forward, "project": task_project, "correct": task_correct, "adam": task_adam, "final": task_final,
    }
    run = set()

    def need(name, i):
        if (name, i) not in run:
            run.add((name, i))
            tasks[name](i)

    for name, i in ORDER:
        need(name, i)
    new_delta, first_new, second_new = got["adam"]
    return (got["projected"], got["input_grad"], new_delta, first_new, second_new)


def solution(mesh):
    placed = (
        P(("dp", "tensor"), None),
        P(None, "tensor"),
        P("dp", "tensor"),
        P(),
        P(),
        P("dp", "tensor"),
        P("dp", "tensor"),
        P("dp", "tensor"),
    )
    return jax.shard_map(
        on_device,
        mesh=mesh,
        in_specs=placed,
        out_specs=(
            P("dp", "tensor"),
            P(("dp", "tensor"), None),
            P("dp", "tensor"),
            P("dp", "tensor"),
            P("dp", "tensor"),
        ),
        check_vma=False,
    )
```
